768 devices in a mesh: fsdp: 64 (over y, x, core), dp: 12 (over z).
Axes of the slice: x: 4, y: 8, z: 12, core: 2. Of those that a mesh axis runs over, the one named last changes fastest.
Arguments:
- grads: bfloat16 [12, 4096, 14336], P('dp', 'fsdp')
- q_prev: float32 [32, 14336], replicated, may hold values from -6 to 6
Outputs:
- q_new: float32 [32, 14336], replicated
- resid_new: bfloat16 [12, 4096, 14336], P('dp', 'fsdp')
The draws below stay inside these ranges and needn't reach their ends.
All inputs are finite; a program needn't handle non-finite values.
Results may differ from the reference program's by a relative error of at most 0.001.
Values sent between devices are 32-bit elements; how exact they have to be, the bound alone decides.
No kernel may reach another device: no remote copies, remote signals or barrier semaphores. Data moves between devices by JAX's collectives and lax.ppermute only.
A program may use at most 64 MiB of HBM per device.

```python
import math
import jax
import jax.numpy as jnp
from jax import lax

ROWS = 4096
COLS = 14336
RANK = 32
GROUPS = 12
N_DP = 12


def draw_grads(key, part):
    key = jax.random.fold_in(key, 11)
    key_base, key_rows, key_cols = jax.random.split(key, 3)
    row_pos = jnp.arange(ROWS).astype(jnp.float32).reshape(1, ROWS, 1)
    row_scale = jnp.exp(jax.random.uniform(key_rows, (GROUPS, ROWS, 1), jnp.float32, 0.0, math.log(10.0)))
    row_scale = row_scale * (1.0 + 2.0 * row_pos / ROWS)
    col_scale = jnp.exp(jax.random.uniform(key_cols, (1, 1, COLS), jnp.float32, 0.0, math.log(10.0)))
    base = jax.random.normal(key_base, (GROUPS, ROWS, COLS), jnp.float32)
    return (0.05 * base * row_scale * col_scale).astype(jnp.bfloat16)


def normal_values(stream_key, shape, spread, limit, kind=jnp.bfloat16):
    return jnp.clip(spread * jax.random.normal(stream_key, shape, jnp.float32), -limit, limit).astype(kind)


def setup_inputs(seed: int = 0) -> dict:
    key_list = jax.random.split(jax.random.key(seed), 3)
    grads = draw_grads(jax.random.fold_in(key_list[2], 71), 0)
    q_prev = normal_values(key_list[1], (RANK, COLS), 1.0, 6.0, jnp.float32)
    return {"grads": grads, "q_prev": q_prev}


HIGH = lax.Precision.HIGHEST

def correct(piece):
    return piece.astype(jnp.float32)

def reference(grads, q_prev):

    def project(piece):
        return lax.dot_general(correct(piece).astype(jnp.float32), q_prev.astype(jnp.float32), (((1,), (1,)), ((), ())), precision=HIGH, preferred_element_type=jnp.float32)
    left = jnp.sum(lax.map(project, grads), axis=0)
    gram = jnp.dot(left.T.astype(jnp.float32), left.astype(jnp.float32), precision=HIGH, preferred_element_type=jnp.float32)
    lower = jnp.linalg.cholesky(gram)
    basis = lax.linalg.triangular_solve(lower, left, left_side=False, lower=True, transpose_a=True)

    def back(piece):
        return lax.dot_general(basis.astype(jnp.float32), correct(piece).astype(jnp.float32), (((0,), (0,)), ((), ())), precision=HIGH, preferred_element_type=jnp.float32)
    q_new = jnp.sum(lax.map(back, grads), axis=0) / N_DP

    def update(piece):
        approx = jnp.dot(basis.astype(jnp.float32), q_new.astype(jnp.float32), precision=HIGH, preferred_element_type=jnp.float32)
        return (correct(piece) - approx).astype(jnp.bfloat16)
    resid_new = lax.map(update, grads)
    return (q_new, resid_new)
```

```python
import jax
import jax.numpy as jnp
from jax import lax
from jax.sharding import Mesh, PartitionSpec as P

HIGH = lax.Precision.HIGHEST
F32 = jnp.float32
NY, NX, NC = 8, 4, 2
TILE = 8
GRAM = 128


def spread(block, axis):
    count = lax.axis_size(axis)
    copies = jnp.broadcast_to(block[None], (count,) + block.shape)
    return lax.all_to_all(copies, axis, 0, 0, tiled=True)


def dot(a, b, contract):
    return lax.dot_general(a, b, ((contract[0:1], contract[1:2]), ((), ())), precision=HIGH, preferred_element_type=F32)


def per_device(grads, q_prev):
    corrected = grads[0].astype(F32)
    rank, cols = q_prev.shape
    rows = corrected.shape[0]
    groups = lax.axis_size("dp")
    wide = cols // (NC * NY)
    core = lax.axis_index("c")

    local = dot(q_prev, corrected, (1, 1))
    local = jnp.concatenate([local[: rank // 2], local[rank // 2 :]], axis=1)
    left_t = jnp.sum(spread(local, "dp"), axis=0)
    left_t = jnp.concatenate([left_t[:, :rows], left_t[:, rows:]], axis=0)

    gram = dot(left_t, left_t, (1, 1))
    gram = gram.reshape(NX, TILE, rank).transpose(1, 0, 2).reshape(TILE, GRAM)
    term = dot(left_t, corrected, (1, 0))
    term = term.reshape(NX, TILE, NC, NY, wide).transpose(2, 0, 3, 1, 4)
    tail = jnp.broadcast_to(gram, (NX, NY, TILE, GRAM))
    first = jnp.concatenate([term[0], tail], axis=-1)
    second = jnp.concatenate([term[1], tail], axis=-1)
    swap = [(0, 1), (1, 0)]
    other = lax.ppermute(jnp.where(core == 0, second, first), "c", swap)
    mine = jnp.where(core == 0, first, second) + other
    mine = mine.reshape(NX * NY, TILE, wide + GRAM)
    mine = jnp.sum(lax.all_to_all(mine, ("x", "y"), 0, 0, tiled=True), axis=0)
    gram = mine[:, wide:].reshape(TILE, NX, rank).transpose(1, 0, 2).reshape(rank, rank)
    block = jnp.sum(spread(mine[:, :wide], "dp"), axis=0)

    block = spread(block, "y")
    block = lax.all_gather(block, "x", axis=0)
    other = lax.ppermute(block, "c", swap)
    first = jnp.where(core == 0, block, other)
    second = jnp.where(core == 0, other, block)
    total = jnp.stack([first, second]).transpose(1, 3, 0, 2, 4).reshape(rank, cols)

    lower = jnp.linalg.cholesky(gram)
    inverse = lax.linalg.triangular_solve(lower, jnp.eye(rank, dtype=F32), left_side=True, lower=True)
    basis = dot(left_t, inverse, (0, 1))
    q_new = dot(inverse, total, (1, 0)) / groups
    resid_new = (corrected - dot(basis, q_new, (1, 0))).astype(jnp.bfloat16)
    return (q_new, resid_new[None])


def solution(mesh):
    groups = mesh.devices.shape[1]
    fine = Mesh(mesh.devices.reshape(NY, NX, NC, groups), ("y", "x", "c", "dp"))
    split = P("dp", ("y", "x", "c"), None)
    return jax.shard_map(per_device, mesh=fine, in_specs=(split, P()), out_specs=(P(), split), check_vma=False)
```

```python
import functools

import jax
import jax.numpy as jnp
from jax import lax
from jax.experimental import pallas as pl
from jax.experimental.pallas import tpu as pltpu
from jax.sharding import Mesh, PartitionSpec as P

HIGH = lax.Precision.HIGHEST
F32, BF16 = jnp.float32, jnp.bfloat16
NY, NX, NC = 8, 4, 2
SUB, LANE = 8, 128
RANK = 32
TILES = 7
STEP = 14
WIDE = STEP * LANE
VMEM = 24 * 1024 * 1024


def params():
    return pltpu.CompilerParams(vmem_limit_bytes=VMEM, dimension_semantics=("arbitrary",))


def pieces(value, count):
    parts = []
    for _ in range(count):
        part = value.astype(BF16)
        parts.append(part)
        value = value - part.astype(F32)
    return parts


def dot(a, b, contract, precision=None):
    dims = ((contract[0:1], contract[1:2]), ((), ()))
    return lax.dot_general(a, b, dims, precision=precision, preferred_element_type=F32)


def left_of(shares_ref):
    packed = shares_ref[0]
    for g in range(1, shares_ref.shape[0]):
        packed = packed + shares_ref[g]
    half = LANE // 2
    return jnp.concatenate([packed[:, :half], packed[:, half:]], axis=0)


def project_kernel(grads_ref, q_ref, out_ref, acc_ref):
    step = pl.program_id(0)
    stack = jnp.concatenate(pieces(q_ref[...], 3), axis=0)
    part = dot(stack, grads_ref[0], (1, 1))

    @pl.when(step == 0)
    def _():
        acc_ref[...] = part

    @pl.when(step > 0)
    def _():
        acc_ref[...] += part

    @pl.when(step == pl.num_programs(0) - 1)
    def _():
        local = acc_ref[0:RANK] + acc_ref[RANK : 2 * RANK] + acc_ref[2 * RANK :]
        packed = jnp.concatenate([local[: RANK // 2], local[RANK // 2 :]], axis=1)
        for g in range(out_ref.shape[0]):
            out_ref[g] = packed


def project(grads, q_prev, groups):
    rows, cols = grads.shape[1:]
    wide = 2 * WIDE
    return pl.pallas_call(
        project_kernel,
        grid=(cols // wide,),
        in_specs=[
            pl.BlockSpec((1, rows, wide), lambda j: (0, 0, j)),
            pl.BlockSpec((RANK, wide), lambda j: (0, j)),
        ],
        out_specs=pl.BlockSpec((groups, RANK // 2, LANE), lambda j: (0, 0, 0)),
        out_shape=jax.ShapeDtypeStruct((groups, RANK // 2, LANE), F32),
        scratch_shapes=[pltpu.VMEM((3 * RANK, rows), F32)],
        compiler_params=params(),
        name="project",
    )(grads, q_prev)


def term_kernel(side_ref, shares_ref, grads_ref, out_ref):
    step = pl.program_id(0)
    left = left_of(shares_ref)
    stack = jnp.concatenate(pieces(left, 3), axis=0)
    part = dot(stack, grads_ref[0], (1, 0))
    part = part[:RANK] + part[RANK : 2 * RANK] + part[2 * RANK :]
    for x in range(NX):
        for t in range(STEP):
            out_ref[x, step * STEP + t] = part[x * SUB : (x + 1) * SUB, t * LANE : (t + 1) * LANE]

    @pl.when(step == 0)
    def _():
        wide = dot(left, jnp.concatenate([left] * NX, axis=0), (1, 1), HIGH)
        slot = lax.broadcasted_iota(jnp.int32, (SUB, LANE), 1) // RANK
        tile = jnp.zeros((SUB, LANE), F32)
        for x in range(NX):
            tile = jnp.where(slot == x, wide[x * SUB : (x + 1) * SUB], tile)
        for x in range(NX):
            out_ref[x, out_ref.shape[1] - 1] = tile


def term(side, shares, grads):
    rows, cols = grads.shape[1:]
    tiles = cols // NC // LANE
    steps = tiles // STEP
    shape = (NX, tiles + 1, SUB, LANE)
    return pl.pallas_call(
        term_kernel,
        grid_spec=pltpu.PrefetchScalarGridSpec(
            num_scalar_prefetch=1,
            grid=(steps,),
            in_specs=[
                pl.BlockSpec(shares.shape, lambda j, side: (0, 0, 0)),
                pl.BlockSpec((1, rows, WIDE), lambda j, side: (0, 0, side[0] * steps + j)),
            ],
            out_specs=pl.BlockSpec(shape, lambda j, side: (0, 0, 0, 0)),
        ),
        out_shape=jax.ShapeDtypeStruct(shape, F32),
        compiler_params=params(),
        cost_estimate=pl.CostEstimate(flops=2 * 96 * rows * cols // NC, bytes_accessed=3 * rows * cols, transcendentals=0),
        name="term",
    )(side, shares, grads)


def factor_kernel(gram_ref, shares_ref, inverse_ref, basis_ref):
    tile = gram_ref[...]
    lane = lax.broadcasted_iota(jnp.int32, (RANK, LANE), 1)
    row = lax.broadcasted_iota(jnp.int32, (RANK, LANE), 0)
    work = jnp.concatenate([pltpu.roll(tile, (LANE - RANK * x) % LANE, 1) for x in range(NX)], axis=0)
    work = jnp.where(lane < RANK, work, jnp.where(lane - RANK == row, 1.0, 0.0))
    for k in range(RANK):
        scale = 1.0 / jnp.sqrt(work[k : k + 1, k : k + 1])
        across = work[k : k + 1] * scale
        down = work[:, k : k + 1] * scale
        work = jnp.where(row > k, work - down * across, jnp.where(row == k, across, work))
    inverse = jnp.where(lane < RANK, pltpu.roll(work, LANE - RANK, 1), 0.0)
    one, two, three = [part.astype(F32) for part in pieces(inverse, 3)]

    def at(value, slot):
        return pltpu.roll(value, RANK * slot, 1) if slot else value

    inverse_ref[:, :LANE] = (at(one, 0) + at(one, 1) + at(two, 2) + at(one, 3)).astype(BF16)
    inverse_ref[:, LANE:] = (at(two, 0) + at(three, 1)).astype(BF16)
    basis = dot(left_of(shares_ref), jnp.concatenate([inverse[:, :RANK]] * 4, axis=0), (0, 1), HIGH)
    high = basis.astype(BF16).astype(F32)
    wide = lax.broadcasted_iota(jnp.int32, basis.shape, 1)
    basis_ref[...] = jnp.where(wide < LANE // 2, high, basis - high).astype(BF16)


def factor(gram, shares, rows):
    return pl.pallas_call(
        factor_kernel,
        out_shape=(
            jax.ShapeDtypeStruct((RANK, 2 * LANE), BF16),
            jax.ShapeDtypeStruct((rows, LANE), BF16),
        ),
        compiler_params=pltpu.CompilerParams(vmem_limit_bytes=VMEM),
        cost_estimate=pl.CostEstimate(flops=1 << 22, bytes_accessed=1 << 20, transcendentals=32),
        name="factor",
    )(gram, shares)


def finish_kernel(groups, side_ref, total_ref, inverse_ref, basis_ref, grads_ref, *rest):
    q_ref, resid_ref = rest[-2:]
    total = jnp.concatenate(
        [jnp.concatenate([total_ref[x, t] for x in range(NX)], axis=0) for t in range(STEP)], axis=1
    )
    one, two, three = pieces(total, 3)
    stack = jnp.concatenate([one, two, one, three, two, one, one, one], axis=0)
    q_new = dot(inverse_ref[...], stack, (1, 0)) / groups
    q_ref[...] = q_new
    high, low = pieces(q_new, 2)
    approx = dot(basis_ref[...], jnp.concatenate([high, low, high, low], axis=0), (1, 0))
    resid_ref[0] = (grads_ref[0].astype(F32) - approx).astype(BF16)


def finish(side, total, inverse, basis, grads, groups, partial=()):
    rows, cols = grads.shape[1:]
    steps = total.shape[1] // STEP
    whole = lambda j, side: (0, 0)
    return pl.pallas_call(
        functools.partial(finish_kernel, groups),
        grid_spec=pltpu.PrefetchScalarGridSpec(
            num_scalar_prefetch=1,
            grid=(steps,),
            in_specs=[
                pl.BlockSpec((NX, STEP, SUB, LANE), lambda j, side: (0, j, 0, 0)),
                pl.BlockSpec(inverse.shape, whole),
                pl.BlockSpec(basis.shape, whole),
                pl.BlockSpec((1, rows, WIDE), lambda j, side: (0, 0, side[0] * steps + j)),
            ]
            + [pl.BlockSpec(memory_space=pl.ANY)] * len(partial),
            out_specs=[
                pl.BlockSpec((RANK, WIDE), lambda j, side: (0, side[0] * steps + j)),
                pl.BlockSpec((1, rows, WIDE), lambda j, side: (0, 0, side[0] * steps + j)),
            ],
        ),
        out_shape=(
            jax.ShapeDtypeStruct((RANK, cols), F32),
            jax.ShapeDtypeStruct((1, rows, cols), BF16),
        ),
        input_output_aliases={5: 0, 6: 1} if partial else {},
        compiler_params=params(),
        cost_estimate=pl.CostEstimate(flops=2 * 160 * rows * cols // NC, bytes_accessed=6 * rows * cols, transcendentals=0),
        name="finish",
    )(side, total, inverse, basis, grads, *partial)


def exchange(blocks, axis):
    return lax.all_to_all(blocks, axis, 0, 0, tiled=True)


def spread(block, axis):
    return exchange(jnp.broadcast_to(block[None], (lax.axis_size(axis),) + block.shape), axis)


def per_device(grads, q_prev):
    groups = lax.axis_size("dp")
    core = lax.axis_index("c").astype(jnp.int32)
    own = core.reshape(1)
    other = 1 - own
    swap = [(0, 1), (1, 0)]

    shares = exchange(project(grads, q_prev, groups), "dp")
    away = lax.ppermute(term(other, shares, grads), "c", swap)
    part = term(own, shares, grads) + away
    part = jnp.sum(exchange(part, "x"), axis=0)
    tail = jnp.broadcast_to(part[-1], (NY, 1, SUB, LANE))
    part = jnp.concatenate([part[:-1].reshape(NY, TILES, SUB, LANE), tail], axis=1)
    part = jnp.sum(exchange(part, "y"), axis=0)
    inverse, basis = factor(part[TILES], shares, grads.shape[1])
    part = jnp.sum(spread(part[:TILES], "dp"), axis=0)

    total = spread(part, "y").reshape(NY * TILES, SUB, LANE)
    total = lax.all_gather(total, "x", axis=0)
    away = lax.ppermute(total, "c", swap)
    mine = finish(own, total, inverse, basis, grads, groups)
    return tuple(finish(other, away, inverse, basis, grads, groups, mine))


def solution(mesh):
    groups = mesh.devices.shape[1]
    fine = Mesh(mesh.devices.reshape(NY, NX, NC, groups), ("y", "x", "c", "dp"))
    split = P("dp", ("y", "x", "c"), None)
    return jax.shard_map(per_device, mesh=fine, in_specs=(split, P()), out_specs=(P(), split), check_vma=False)
```

```python
import functools

import jax
import jax.numpy as jnp
from jax import lax
from jax.experimental import pallas as pl
from jax.experimental.pallas import tpu as pltpu
from jax.sharding import Mesh, PartitionSpec as P

HIGH = lax.Precision.HIGHEST
F32, BF16 = jnp.float32, jnp.bfloat16
NY, NX, NC = 8, 4, 2
SUB, LANE = 8, 128
RANK = 32
TILES = 7
STEP = 28
WIDE = STEP * LANE
COPIES = 2
AHEAD = 4
VMEM = 24 * 1024 * 1024


def params():
    return pltpu.CompilerParams(vmem_limit_bytes=VMEM, dimension_semantics=("arbitrary",))


def pieces(value, count):
    parts = []
    for _ in range(count):
        part = value.astype(BF16)
        parts.append(part)
        value = value - part.astype(F32)
    return parts


def dot(a, b, contract, precision=None):
    dims = ((contract[0:1], contract[1:2]), ((), ()))
    return lax.dot_general(a, b, dims, precision=precision, preferred_element_type=F32)


def left_of(shares_ref):
    packed = shares_ref[0]
    for g in range(1, shares_ref.shape[0]):
        packed = packed + shares_ref[g]
    half = LANE // 2
    return jnp.concatenate([packed[:, :half], packed[:, half:]], axis=0)


def project_kernel(own_ref, grads_ref, q_ref, out_ref, grads_buf, sides_ref, q_buf, sems):
    sides_ref[0] = own_ref[0]
    sides_ref[1] = 1 - own_ref[0]
    count = sems.shape[0]
    wide = q_buf.shape[1] // count
    copies = []
    for n in range(count):
        cols = pl.ds(n * wide, wide)
        copies.append(
            (
                pltpu.make_async_copy(grads_ref.at[:, :, cols], grads_buf.at[:, :, cols], sems.at[n, 0]),
                pltpu.make_async_copy(q_ref.at[:, cols], q_buf.at[:, cols], sems.at[n, 1]),
            )
        )
        for copy in copies[-1]:
            copy.start()
    total = None
    for n in range(count):
        for copy in copies[n]:
            copy.wait()
        cols = pl.ds(n * wide, wide)
        stack = jnp.concatenate(pieces(q_buf[:, cols], 3), axis=0)
        part = dot(stack, grads_buf[0, :, cols], (1, 1))
        total = part if total is None else total + part
    local = total[:RANK] + total[RANK : 2 * RANK] + total[2 * RANK :]
    packed = jnp.concatenate([local[: RANK // 2], local[RANK // 2 :]], axis=1)
    for g in range(out_ref.shape[0]):
        out_ref[g] = packed


def project(own, grads, q_prev, groups):
    rows, cols = grads.shape[1:]
    return pl.pallas_call(
        project_kernel,
        in_specs=[pl.BlockSpec(memory_space=pltpu.SMEM)] + [pl.BlockSpec(memory_space=pl.ANY)] * 2,
        out_specs=(
            pl.BlockSpec(memory_space=pltpu.VMEM),
            pl.BlockSpec(memory_space=pltpu.VMEM),
            pl.BlockSpec(memory_space=pltpu.SMEM),
        ),
        out_shape=(
            jax.ShapeDtypeStruct((groups, RANK // 2, LANE), F32),
            pltpu.VMEM(grads.shape, BF16),
            jax.ShapeDtypeStruct((2,), jnp.int32),
        ),
        scratch_shapes=[
            pltpu.VMEM((RANK, cols), F32),
            pltpu.SemaphoreType.DMA((COPIES, 2)),
        ],
        compiler_params=pltpu.CompilerParams(vmem_limit_bytes=VMEM),
        name="project",
    )(own, pltpu.with_memory_space_constraint(grads, pltpu.HBM), pltpu.with_memory_space_constraint(q_prev, pltpu.HBM))


def term_kernel(sides_ref, shares_ref, grads_ref, out_ref):
    left = left_of(shares_ref)
    stack = jnp.concatenate(pieces(left, 3), axis=0)
    part = dot(stack, grads_ref[0], (1, 0))
    part = part[:RANK] + part[RANK : 2 * RANK] + part[2 * RANK :]
    tiles = out_ref.shape[1] - 1
    wide = dot(left, jnp.concatenate([left] * NX, axis=0), (1, 1), HIGH)
    slot = lax.broadcasted_iota(jnp.int32, (SUB, LANE), 1) // RANK
    tile = jnp.zeros((SUB, LANE), F32)
    for x in range(NX):
        tile = jnp.where(slot == x, wide[x * SUB : (x + 1) * SUB], tile)
    for x in range(NX):
        for t in range(tiles):
            out_ref[x, t] = part[x * SUB : (x + 1) * SUB, t * LANE : (t + 1) * LANE]
        out_ref[x, tiles] = tile


def term(side, sides, shares, grads):
    rows, cols = grads.shape[1:]
    half = cols // NC
    shape = (NX, half // LANE + 1, SUB, LANE)
    return pl.pallas_call(
        term_kernel,
        grid_spec=pltpu.PrefetchScalarGridSpec(
            num_scalar_prefetch=1,
            grid=(1,),
            in_specs=[
                pl.BlockSpec(shares.shape, lambda j, sides: (0, 0, 0)),
                pl.BlockSpec((1, rows, half), lambda j, sides: (0, 0, sides[side])),
            ],
            out_specs=pl.BlockSpec(shape, lambda j, sides: (0, 0, 0, 0)),
        ),
        out_shape=jax.ShapeDtypeStruct(shape, F32),
        compiler_params=params(),
        cost_estimate=pl.CostEstimate(flops=2 * 96 * rows * half, bytes_accessed=6 * rows * half, transcendentals=0),
        name="term",
    )(sides, shares, grads)


def factor_kernel(gram_ref, shares_ref, inverse_ref, basis_ref):
    tile = gram_ref[...]
    lane = lax.broadcasted_iota(jnp.int32, (RANK, LANE), 1)
    row = lax.broadcasted_iota(jnp.int32, (RANK, LANE), 0)
    work = jnp.concatenate([pltpu.roll(tile, (LANE - RANK * x) % LANE, 1) for x in range(NX)], axis=0)
    work = jnp.where(lane < RANK, work, jnp.where(lane - RANK == row, 1.0, 0.0))
    for k in range(0, RANK, AHEAD):
        downs = [jnp.broadcast_to(work[:, j : j + 1], work.shape) for j in range(k, k + AHEAD)]
        rights = [work[j : j + 1] for j in range(k, k + AHEAD)]
        for j in range(AHEAD):
            down = downs[j]
            scale = 1.0 / down[k + j : k + j + 1]
            across = rights[j] * scale
            for i in range(j + 1, AHEAD):
                ratio = down[k + i : k + i + 1]
                rights[i] = rights[i] - ratio * across
                downs[i] = downs[i] - down * (ratio * scale)
            work = jnp.where(row > k + j, work - down * across, work)
    pivots = jnp.sum(jnp.where(lane == row, work, 0.0), axis=1, keepdims=True)
    work = work * (1.0 / jnp.sqrt(pivots))
    inverse = jnp.where(lane < RANK, pltpu.roll(work, LANE - RANK, 1), 0.0)
    one, two, three = [part.astype(F32) for part in pieces(inverse, 3)]

    def at(value, slot):
        return pltpu.roll(value, RANK * slot, 1) if slot else value

    inverse_ref[:, :LANE] = (at(one, 0) + at(one, 1) + at(two, 2) + at(one, 3)).astype(BF16)
    inverse_ref[:, LANE:] = (at(two, 0) + at(three, 1)).astype(BF16)
    basis = dot(left_of(shares_ref), jnp.concatenate([inverse[:, :RANK]] * 4, axis=0), (0, 1), HIGH)
    high = basis.astype(BF16).astype(F32)
    wide = lax.broadcasted_iota(jnp.int32, basis.shape, 1)
    basis_ref[...] = jnp.where(wide < LANE // 2, high, basis - high).astype(BF16)


def factor(gram, shares, rows):
    return pl.pallas_call(
        factor_kernel,
        out_shape=(
            jax.ShapeDtypeStruct((RANK, 2 * LANE), BF16),
            jax.ShapeDtypeStruct((rows, LANE), BF16),
        ),
        compiler_params=pltpu.CompilerParams(vmem_limit_bytes=VMEM),
        cost_estimate=pl.CostEstimate(flops=1 << 22, bytes_accessed=1 << 20, transcendentals=32),
        name="factor",
    )(gram, shares)


def finish_kernel(groups, sides_ref, total_ref, inverse_ref, basis_ref, grads_ref, *rest):
    q_ref, resid_ref = rest[-2:]
    total = jnp.concatenate(
        [jnp.concatenate([total_ref[x, t] for x in range(NX)], axis=0) for t in range(STEP)], axis=1
    )
    one, two, three = pieces(total, 3)
    stack = jnp.concatenate([one, two, one, three, two, one, one, one], axis=0)
    q_new = dot(inverse_ref[...], stack, (1, 0)) / groups
    q_ref[...] = q_new
    high, low = pieces(q_new, 2)
    approx = dot(basis_ref[...], jnp.concatenate([high, low, high, low], axis=0), (1, 0))
    resid_ref[0] = (grads_ref[0].astype(F32) - approx).astype(BF16)


def finish(side, sides, total, inverse, basis, grads, groups, partial=()):
    rows, cols = grads.shape[1:]
    steps = total.shape[1] // STEP
    whole = lambda j, sides: (0, 0)
    return pl.pallas_call(
        functools.partial(finish_kernel, groups),
        grid_spec=pltpu.PrefetchScalarGridSpec(
            num_scalar_prefetch=1,
            grid=(steps,),
            in_specs=[
                pl.BlockSpec((NX, STEP, SUB, LANE), lambda j, sides: (0, j, 0, 0)),
                pl.BlockSpec(inverse.shape, whole),
                pl.BlockSpec(basis.shape, whole),
                pl.BlockSpec((1, rows, WIDE), lambda j, sides: (0, 0, sides[side] * steps + j)),
            ]
            + [pl.BlockSpec(memory_space=pl.ANY)] * len(partial),
            out_specs=[
                pl.BlockSpec((RANK, WIDE), lambda j, sides: (0, sides[side] * steps + j)),
                pl.BlockSpec((1, rows, WIDE), lambda j, sides: (0, 0, sides[side] * steps + j)),
            ],
        ),
        out_shape=(
            jax.ShapeDtypeStruct((RANK, cols), F32),
            jax.ShapeDtypeStruct((1, rows, cols), BF16),
        ),
        input_output_aliases={5: 0, 6: 1} if partial else {},
        compiler_params=params(),
        cost_estimate=pl.CostEstimate(flops=2 * 160 * rows * cols // NC, bytes_accessed=6 * rows * cols, transcendentals=0),
        name="finish",
    )(sides, total, inverse, basis, grads, *partial)


def exchange(blocks, axis):
    return lax.all_to_all(blocks, axis, 0, 0, tiled=True)


def spread(block, axis):
    return exchange(jnp.broadcast_to(block[None], (lax.axis_size(axis),) + block.shape), axis)


def per_device(grads, q_prev):
    groups = lax.axis_size("dp")
    swap = [(0, 1), (1, 0)]

    own = lax.axis_index("c").astype(jnp.int32).reshape(1)
    shares, grads, sides = project(own, grads, q_prev, groups)
    shares = exchange(shares, "dp")
    away = lax.ppermute(term(1, sides, shares, grads), "c", swap)
    part = term(0, sides, shares, grads) + away
    part = jnp.sum(exchange(part, "x"), axis=0)
    tail = jnp.broadcast_to(part[-1], (NY, 1, SUB, LANE))
    part = jnp.concatenate([part[:-1].reshape(NY, TILES, SUB, LANE), tail], axis=1)
    part = jnp.sum(exchange(part, "y"), axis=0)
    inverse, basis = factor(part[TILES], shares, grads.shape[1])
    part = jnp.sum(spread(part[:TILES], "dp"), axis=0)

    total = spread(part, "y").reshape(NY * TILES, SUB, LANE)
    total = lax.all_gather(total, "x", axis=0)
    away = lax.ppermute(total, "c", swap)
    mine = finish(0, sides, total, inverse, basis, grads, groups)
    return tuple(finish(1, sides, away, inverse, basis, grads, groups, mine))


def solution(mesh):
    groups = mesh.devices.shape[1]
    fine = Mesh(mesh.devices.reshape(NY, NX, NC, groups), ("y", "x", "c", "dp"))
    split = P("dp", ("y", "x", "c"), None)
    return jax.shard_map(per_device, mesh=fine, in_specs=(split, P()), out_specs=(P(), split), check_vma=False)
```

```python
import functools

import jax
import jax.numpy as jnp
from jax import lax
from jax.experimental import pallas as pl
from jax.experimental.pallas import tpu as pltpu
from jax.sharding import Mesh, PartitionSpec as P

HIGH = lax.Precision.HIGHEST
F32, BF16 = jnp.float32, jnp.bfloat16
NY, NX, NC, NP = 8, 4, 2, 2
SUB, LANE = 8, 128
RANK = 32
TILES = 4
STEP = 14
WIDE = STEP * LANE
COPIES = 2
AHEAD = 4
VMEM = 24 * 1024 * 1024


def pieces(value, count):
    parts = []
    for _ in range(count):
        part = value.astype(BF16)
        parts.append(part)
        value = value - part.astype(F32)
    return parts


def dot(a, b, contract, precision=None):
    dims = ((contract[0:1], contract[1:2]), ((), ()))
    return lax.dot_general(a, b, dims, precision=precision, preferred_element_type=F32)


def left_of(shares_ref):
    packed = shares_ref[0]
    for g in range(1, shares_ref.shape[0]):
        packed = packed + shares_ref[g]
    half = LANE // 2
    return jnp.concatenate([packed[:, :half], packed[:, half:]], axis=0)


def project_kernel(own_ref, grads_ref, q_ref, out_ref, grads_buf, sides_ref, q_buf, sems):
    sides_ref[0] = own_ref[0]
    sides_ref[1] = 1 - own_ref[0]
    count = sems.shape[0]
    wide = q_buf.shape[1] // count
    copies = []
    for n in range(count):
        cols = pl.ds(n * wide, wide)
        copies.append(
            (
                pltpu.make_async_copy(grads_ref.at[:, :, cols], grads_buf.at[:, :, cols], sems.at[n, 0]),
                pltpu.make_async_copy(q_ref.at[:, cols], q_buf.at[:, cols], sems.at[n, 1]),
            )
        )
        for copy in copies[-1]:
            copy.start()
    total = None
    for n in range(count):
        for copy in copies[n]:
            copy.wait()
        cols = pl.ds(n * wide, wide)
        stack = jnp.concatenate(pieces(q_buf[:, cols], 3), axis=0)
        part = dot(stack, grads_buf[0, :, cols], (1, 1))
        total = part if total is None else total + part
    local = total[:RANK] + total[RANK : 2 * RANK] + total[2 * RANK :]
    packed = jnp.concatenate([local[: RANK // 2], local[RANK // 2 :]], axis=1)
    for g in range(out_ref.shape[0]):
        out_ref[g] = packed


def project(own, grads, q_prev, groups):
    rows, cols = grads.shape[1:]
    return pl.pallas_call(
        project_kernel,
        in_specs=[pl.BlockSpec(memory_space=pltpu.SMEM)] + [pl.BlockSpec(memory_space=pl.ANY)] * 2,
        out_specs=(
            pl.BlockSpec(memory_space=pltpu.VMEM),
            pl.BlockSpec(memory_space=pltpu.VMEM),
            pl.BlockSpec(memory_space=pltpu.SMEM),
        ),
        out_shape=(
            jax.ShapeDtypeStruct((groups, RANK // 2, LANE), F32),
            pltpu.VMEM(grads.shape, BF16),
            jax.ShapeDtypeStruct((2,), jnp.int32),
        ),
        scratch_shapes=[
            pltpu.VMEM((RANK, cols), F32),
            pltpu.SemaphoreType.DMA((COPIES, 2)),
        ],
        compiler_params=pltpu.CompilerParams(vmem_limit_bytes=VMEM),
        name="project",
    )(own, pltpu.with_memory_space_constraint(grads, pltpu.HBM), pltpu.with_memory_space_constraint(q_prev, pltpu.HBM))


def term_kernel(sides_ref, shares_ref, grads_ref, out_ref):
    left = left_of(shares_ref)
    stack = jnp.concatenate(pieces(left, 3), axis=0)
    part = dot(stack, grads_ref[0], (1, 0))
    part = part[:RANK] + part[RANK : 2 * RANK] + part[2 * RANK :]
    tiles = out_ref.shape[1] - 1
    wide = dot(left, jnp.concatenate([left] * NX, axis=0), (1, 1), HIGH)
    slot = lax.broadcasted_iota(jnp.int32, (SUB, LANE), 1) // RANK
    tile = jnp.zeros((SUB, LANE), F32)
    for x in range(NX):
        tile = jnp.where(slot == x, wide[x * SUB : (x + 1) * SUB], tile)
    for x in range(NX):
        for p in range(NP):
            for t in range(tiles):
                cols = slice((p * tiles + t) * LANE, (p * tiles + t + 1) * LANE)
                out_ref[x * NP + p, t] = part[x * SUB : (x + 1) * SUB, cols]
            out_ref[x * NP + p, tiles] = tile


def term(side, sides, shares, grads):
    rows, cols = grads.shape[1:]
    half = cols // NC
    shape = (NX * NP, half // NP // LANE + 1, SUB, LANE)
    return pl.pallas_call(
        term_kernel,
        grid_spec=pltpu.PrefetchScalarGridSpec(
            num_scalar_prefetch=1,
            grid=(1,),
            in_specs=[
                pl.BlockSpec(shares.shape, lambda j, sides: (0, 0, 0)),
                pl.BlockSpec((1, rows, half), lambda j, sides: (0, 0, sides[side])),
            ],
            out_specs=pl.BlockSpec(shape, lambda j, sides: (0, 0, 0, 0)),
        ),
        out_shape=jax.ShapeDtypeStruct(shape, F32),
        compiler_params=pltpu.CompilerParams(vmem_limit_bytes=VMEM),
        cost_estimate=pl.CostEstimate(flops=2 * 96 * rows * half, bytes_accessed=6 * rows * half, transcendentals=0),
        name="term",
    )(sides, shares, grads)


def factor_kernel(gram_ref, shares_ref, inverse_ref, basis_ref):
    tile = gram_ref[...] / shares_ref.shape[0]
    lane = lax.broadcasted_iota(jnp.int32, (RANK, LANE), 1)
    row = lax.broadcasted_iota(jnp.int32, (RANK, LANE), 0)
    work = jnp.concatenate([pltpu.roll(tile, (LANE - RANK * x) % LANE, 1) for x in range(NX)], axis=0)
    work = jnp.where(lane < RANK, work, jnp.where(lane - RANK == row, 1.0, 0.0))
    for k in range(0, RANK, AHEAD):
        downs = [jnp.broadcast_to(work[:, j : j + 1], work.shape) for j in range(k, k + AHEAD)]
        rights = [work[j : j + 1] for j in range(k, k + AHEAD)]
        for j in range(AHEAD):
            down = downs[j]
            scale = 1.0 / down[k + j : k + j + 1]
            across = rights[j] * scale
            for i in range(j + 1, AHEAD):
                ratio = down[k + i : k + i + 1]
                rights[i] = rights[i] - ratio * across
                downs[i] = downs[i] - down * (ratio * scale)
            work = jnp.where(row > k + j, work - down * across, work)
    pivots = jnp.sum(jnp.where(lane == row, work, 0.0), axis=1, keepdims=True)
    work = work * (1.0 / jnp.sqrt(pivots))
    inverse = jnp.where(lane < RANK, pltpu.roll(work, LANE - RANK, 1), 0.0)
    one, two, three = [part.astype(F32) for part in pieces(inverse, 3)]

    def at(value, slot):
        return pltpu.roll(value, RANK * slot, 1) if slot else value

    inverse_ref[:, :LANE] = (at(one, 0) + at(one, 1) + at(two, 2) + at(one, 3)).astype(BF16)
    inverse_ref[:, LANE:] = (at(two, 0) + at(three, 1)).astype(BF16)
    basis = dot(left_of(shares_ref), jnp.concatenate([inverse[:, :RANK]] * 4, axis=0), (0, 1), HIGH)
    high = basis.astype(BF16).astype(F32)
    wide = lax.broadcasted_iota(jnp.int32, basis.shape, 1)
    basis_ref[...] = jnp.where(wide < LANE // 2, high, basis - high).astype(BF16)


def factor(gram, shares, rows):
    return pl.pallas_call(
        factor_kernel,
        out_shape=(
            jax.ShapeDtypeStruct((RANK, 2 * LANE), BF16),
            jax.ShapeDtypeStruct((rows, LANE), BF16),
        ),
        compiler_params=pltpu.CompilerParams(vmem_limit_bytes=VMEM),
        cost_estimate=pl.CostEstimate(flops=1 << 22, bytes_accessed=1 << 20, transcendentals=32),
        name="factor",
    )(gram, shares)


def finish_kernel(groups, side, sides_ref, total_ref, inverse_ref, basis_ref, grads_ref, *rest):
    q_ref, resid_ref, q_buf, resid_buf, sems = rest[-5:]
    tiles = total_ref.shape[1] - 1
    copies = []
    for n in range(sems.shape[0]):
        here = pl.ds(n * WIDE, WIDE)
        there = pl.ds(pl.multiple_of(sides_ref[side] * q_buf.shape[1] + n * WIDE, LANE), WIDE)
        columns = []
        for t in range(n * STEP, (n + 1) * STEP):
            parts = [total_ref[x * NP + t // tiles, t % tiles] for x in range(NX)]
            columns.append(jnp.concatenate(parts, axis=0))
        one, two, three = pieces(jnp.concatenate(columns, axis=1), 3)
        stack = jnp.concatenate([one, two, one, three, two, one, one, one], axis=0)
        q_new = dot(inverse_ref[...], stack, (1, 0)) / groups
        q_buf[:, here] = q_new
        copies.append(pltpu.make_async_copy(q_buf.at[:, here], q_ref.at[:, there], sems.at[n, 0]))
        copies[-1].start()
        high, low = pieces(q_new, 2)
        approx = dot(basis_ref[...], jnp.concatenate([high, low, high, low], axis=0), (1, 0))
        resid_buf[0, :, here] = (grads_ref[0, :, there].astype(F32) - approx).astype(BF16)
        copies.append(pltpu.make_async_copy(resid_buf.at[:, :, here], resid_ref.at[:, :, there], sems.at[n, 1]))
        copies[-1].start()
    for copy in copies:
        copy.wait()


def finish(side, sides, total, inverse, basis, grads, groups, partial=()):
    rows, cols = grads.shape[1:]
    half = cols // NC
    return pl.pallas_call(
        functools.partial(finish_kernel, groups, side),
        in_specs=[pl.BlockSpec(memory_space=pltpu.SMEM)]
        + [pl.BlockSpec(memory_space=pltpu.VMEM)] * 4
        + [pl.BlockSpec(memory_space=pl.ANY)] * len(partial),
        out_specs=(pl.BlockSpec(memory_space=pl.ANY),) * 2,
        out_shape=(
            jax.ShapeDtypeStruct((RANK, cols), F32),
            jax.ShapeDtypeStruct((1, rows, cols), BF16),
        ),
        scratch_shapes=[
            pltpu.VMEM((RANK, half), F32),
            pltpu.VMEM((1, rows, half), BF16),
            pltpu.SemaphoreType.DMA((half // WIDE, 2)),
        ],
        input_output_aliases={5: 0, 6: 1} if partial else {},
        compiler_params=pltpu.CompilerParams(vmem_limit_bytes=VMEM),
        cost_estimate=pl.CostEstimate(flops=2 * 160 * rows * half, bytes_accessed=6 * rows * half, transcendentals=0),
        name="finish",
    )(sides, total, inverse, basis, grads, *partial)


def exchange(blocks, axis):
    return lax.all_to_all(blocks, axis, 0, 0, tiled=True)


def spread(block, axis):
    return exchange(jnp.broadcast_to(block[None], (lax.axis_size(axis),) + block.shape), axis)


def per_device(grads, q_prev):
    groups = lax.axis_size(("far", "near"))
    swap = [(0, 1), (1, 0)]
    own = lax.axis_index("c").astype(jnp.int32).reshape(1)

    shares, grads, sides = project(own, grads, q_prev, groups)
    shares = exchange(shares, ("far", "near"))
    away = lax.ppermute(term(1, sides, shares, grads), "c", swap)
    part = term(0, sides, shares, grads) + away
    used = part.shape[1]
    part = jnp.sum(exchange(part, ("x", "near")), axis=0)
    part = jnp.pad(part, ((0, NY * TILES - used), (0, 0), (0, 0)))
    part = jnp.sum(exchange(part.reshape(NY, TILES, SUB, LANE), "y"), axis=0)
    part = jnp.sum(spread(part, "far"), axis=0)

    total = spread(part, "y").reshape(NY * TILES, SUB, LANE)[:used]
    total = spread(total, ("x", "near"))
    away = lax.ppermute(total, "c", swap)
    inverse, basis = factor(total[0, used - 1], shares, grads.shape[1])
    mine = finish(0, sides, total, inverse, basis, grads, groups)
    return tuple(finish(1, sides, away, inverse, basis, grads, groups, mine))


def solution(mesh):
    groups = mesh.devices.shape[1]
    fine = Mesh(mesh.devices.reshape(NY, NX, NC, groups // NP, NP), ("y", "x", "c", "far", "near"))
    split = P(("far", "near"), ("y", "x", "c"), None)
    return jax.shard_map(per_device, mesh=fine, in_specs=(split, P()), out_specs=(P(), split), check_vma=False)
```

```python
import functools

import jax
import jax.numpy as jnp
from jax import lax
from jax.experimental import pallas as pl
from jax.experimental.pallas import tpu as pltpu
from jax.sharding import Mesh, PartitionSpec as P

HIGH = lax.Precision.HIGHEST
F32, BF16 = jnp.float32, jnp.bfloat16
NY, NX, NC, NP = 8, 4, 2, 2
SUB, LANE = 8, 128
RANK = 32
TILES = 4
COPIES = 2
AHEAD = 4
VMEM = 24 * 1024 * 1024


def pieces(value, count):
    parts = []
    for _ in range(count):
        part = value.astype(BF16)
        parts.append(part)
        value = value - part.astype(F32)
    return parts


def dot(a, b, contract, precision=None):
    dims = ((contract[0:1], contract[1:2]), ((), ()))
    return lax.dot_general(a, b, dims, precision=precision, preferred_element_type=F32)


def left_of(shares_ref):
    packed = shares_ref[0]
    for g in range(1, shares_ref.shape[0]):
        packed = packed + shares_ref[g]
    half = LANE // 2
    return jnp.concatenate([packed[:, :half], packed[:, half:]], axis=0)


def project_kernel(own_ref, grads_ref, q_ref, out_ref, grads_buf, sides_ref, q_buf, sems):
    sides_ref[0] = own_ref[0]
    sides_ref[1] = 1 - own_ref[0]
    count = sems.shape[0]
    wide = q_buf.shape[1] // count
    copies = []
    for n in range(count):
        cols = pl.ds(n * wide, wide)
        copies.append(
            (
                pltpu.make_async_copy(grads_ref.at[:, :, cols], grads_buf.at[:, :, cols], sems.at[n, 0]),
                pltpu.make_async_copy(q_ref.at[:, cols], q_buf.at[:, cols], sems.at[n, 1]),
            )
        )
        for copy in copies[-1]:
            copy.start()
    total = None
    for n in range(count):
        for copy in copies[n]:
            copy.wait()
        cols = pl.ds(n * wide, wide)
        stack = jnp.concatenate(pieces(q_buf[:, cols], 2), axis=0)
        part = dot(stack, grads_buf[0, :, cols], (1, 1))
        total = part if total is None else total + part
    local = total[:RANK] + total[RANK:]
    packed = jnp.concatenate([local[: RANK // 2], local[RANK // 2 :]], axis=1)
    for g in range(out_ref.shape[0]):
        out_ref[g] = packed


def project(own, grads, q_prev, groups):
    rows, cols = grads.shape[1:]
    return pl.pallas_call(
        project_kernel,
        in_specs=[pl.BlockSpec(memory_space=pltpu.SMEM)] + [pl.BlockSpec(memory_space=pl.ANY)] * 2,
        out_specs=(
            pl.BlockSpec(memory_space=pltpu.VMEM),
            pl.BlockSpec(memory_space=pltpu.VMEM),
            pl.BlockSpec(memory_space=pltpu.SMEM),
        ),
        out_shape=(
            jax.ShapeDtypeStruct((groups, RANK // 2, LANE), F32),
            pltpu.VMEM(grads.shape, BF16),
            jax.ShapeDtypeStruct((2,), jnp.int32),
        ),
        scratch_shapes=[
            pltpu.VMEM((RANK, cols), F32),
            pltpu.SemaphoreType.DMA((COPIES, 2)),
        ],
        compiler_params=pltpu.CompilerParams(vmem_limit_bytes=VMEM),
        name="project",
    )(own, pltpu.with_memory_space_constraint(grads, pltpu.HBM), pltpu.with_memory_space_constraint(q_prev, pltpu.HBM))


def term_kernel(side, sides_ref, shares_ref, grads_ref, out_ref):
    left = left_of(shares_ref)
    stack = jnp.concatenate(pieces(left, 2), axis=0)
    half = grads_ref.shape[2] // NC
    part = dot(stack, grads_ref[0, :, half_of(side, sides_ref, half)], (1, 0))
    part = part[:RANK] + part[RANK:]
    tiles = out_ref.shape[1] - 1
    wide = dot(left, jnp.concatenate([left] * NX, axis=0), (1, 1), HIGH) / shares_ref.shape[0]
    slot = lax.broadcasted_iota(jnp.int32, (SUB, LANE), 1) // RANK
    tile = jnp.zeros((SUB, LANE), F32)
    for x in range(NX):
        tile = jnp.where(slot == x, wide[x * SUB : (x + 1) * SUB], tile)
    for x in range(NX):
        for p in range(NP):
            for t in range(tiles):
                cols = slice((p * tiles + t) * LANE, (p * tiles + t + 1) * LANE)
                out_ref[x * NP + p, t] = part[x * SUB : (x + 1) * SUB, cols]
            out_ref[x * NP + p, tiles] = tile


def term(side, sides, shares, grads):
    rows, cols = grads.shape[1:]
    half = cols // NC
    shape = (NX * NP, half // NP // LANE + 1, SUB, LANE)
    return pl.pallas_call(
        functools.partial(term_kernel, side),
        in_specs=[pl.BlockSpec(memory_space=pltpu.SMEM)] + [pl.BlockSpec(memory_space=pltpu.VMEM)] * 2,
        out_specs=pl.BlockSpec(memory_space=pltpu.VMEM),
        out_shape=jax.ShapeDtypeStruct(shape, F32),
        compiler_params=pltpu.CompilerParams(vmem_limit_bytes=VMEM),
        cost_estimate=pl.CostEstimate(flops=2 * 96 * rows * half, bytes_accessed=6 * rows * half, transcendentals=0),
        name="term",
    )(sides, shares, grads)


def factor_kernel(gram_ref, shares_ref, inverse_ref, basis_ref):
    tile = gram_ref[...]
    lane = lax.broadcasted_iota(jnp.int32, (RANK, LANE), 1)
    row = lax.broadcasted_iota(jnp.int32, (RANK, LANE), 0)
    work = jnp.concatenate([pltpu.roll(tile, (LANE - RANK * x) % LANE, 1) for x in range(NX)], axis=0)
    work = jnp.where(lane < RANK, work, jnp.where(lane - RANK == row, 1.0, 0.0))
    for k in range(0, RANK, AHEAD):
        downs = [jnp.broadcast_to(work[:, j : j + 1], work.shape) for j in range(k, k + AHEAD)]
        rights = [work[j : j + 1] for j in range(k, k + AHEAD)]
        for j in range(AHEAD):
            down = downs[j]
            scale = 1.0 / down[k + j : k + j + 1]
            across = rights[j] * scale
            for i in range(j + 1, AHEAD):
                ratio = down[k + i : k + i + 1]
                rights[i] = rights[i] - ratio * across
                downs[i] = downs[i] - down * (ratio * scale)
            work = jnp.where(row > k + j, work - down * across, work)
    pivots = jnp.sum(jnp.where(lane == row, work, 0.0), axis=1, keepdims=True)
    work = work * (1.0 / jnp.sqrt(pivots))
    inverse = jnp.where(lane < RANK, pltpu.roll(work, LANE - RANK, 1), 0.0)
    one, two = [part.astype(F32) for part in pieces(inverse, 2)]
    one = one + pltpu.roll(one, RANK, 1)
    two = two + pltpu.roll(two, RANK, 1)
    inverse_ref[...] = (one + pltpu.roll(two, 2 * RANK, 1)).astype(BF16)
    basis = dot(left_of(shares_ref), jnp.concatenate([inverse[:, :RANK]] * 4, axis=0), (0, 1), HIGH)
    high = basis.astype(BF16).astype(F32)
    wide = lax.broadcasted_iota(jnp.int32, basis.shape, 1)
    basis_ref[...] = jnp.where(wide < LANE // 2, high, basis - high).astype(BF16)


def factor(gram, shares, rows):
    return pl.pallas_call(
        factor_kernel,
        out_shape=(
            jax.ShapeDtypeStruct((RANK, LANE), BF16),
            jax.ShapeDtypeStruct((rows, LANE), BF16),
        ),
        compiler_params=pltpu.CompilerParams(vmem_limit_bytes=VMEM),
        cost_estimate=pl.CostEstimate(flops=1 << 22, bytes_accessed=1 << 20, transcendentals=32),
        name="factor",
    )(gram, shares)


def solve(total_ref, inverse_ref, groups):
    tiles = total_ref.shape[1] - 1
    columns = []
    for t in range(NP * tiles):
        parts = [total_ref[x * NP + t // tiles, t % tiles] for x in range(NX)]
        columns.append(jnp.concatenate(parts, axis=0))
    one, two = pieces(jnp.concatenate(columns, axis=1), 2)
    return dot(inverse_ref[...], jnp.concatenate([one, two, one, two], axis=0), (1, 0)) / groups


def residual(q_new, basis_ref, grads):
    high, low = pieces(q_new, 2)
    approx = dot(basis_ref[...], jnp.concatenate([high, low, high, low], axis=0), (1, 0))
    return (grads.astype(F32) - approx).astype(BF16)


def half_of(side, sides_ref, half):
    return pl.ds(pl.multiple_of(sides_ref[side] * half, LANE), half)


def mine_kernel(groups, sides_ref, total_ref, inverse_ref, basis_ref, grads_ref, q_ref, resid_ref):
    q_new = solve(total_ref, inverse_ref, groups)
    q_ref[...] = q_new
    resid_ref[0] = residual(q_new, basis_ref, grads_ref[0, :, half_of(0, sides_ref, q_ref.shape[1])])


def mine(sides, total, inverse, basis, grads, groups):
    rows, cols = grads.shape[1:]
    half = cols // NC
    return pl.pallas_call(
        functools.partial(mine_kernel, groups),
        in_specs=[pl.BlockSpec(memory_space=pltpu.SMEM)] + [pl.BlockSpec(memory_space=pltpu.VMEM)] * 4,
        out_specs=(pl.BlockSpec(memory_space=pltpu.VMEM),) * 2,
        out_shape=(pltpu.VMEM((RANK, half), F32), pltpu.VMEM((1, rows, half), BF16)),
        compiler_params=pltpu.CompilerParams(vmem_limit_bytes=VMEM),
        cost_estimate=pl.CostEstimate(flops=2 * 160 * rows * half, bytes_accessed=6 * rows * half, transcendentals=0),
        name="mine",
    )(sides, total, inverse, basis, grads)


def finish_kernel(
    groups, sides_ref, total_ref, inverse_ref, basis_ref, grads_ref, mine_q_ref, mine_resid_ref,
    q_ref, resid_ref, q_buf, resid_buf, sems,
):
    half = q_buf.shape[1]
    here, there = half_of(0, sides_ref, half), half_of(1, sides_ref, half)
    copies = [
        pltpu.make_async_copy(mine_q_ref, q_ref.at[:, here], sems.at[0]),
        pltpu.make_async_copy(mine_resid_ref, resid_ref.at[:, :, here], sems.at[1]),
        pltpu.make_async_copy(q_buf, q_ref.at[:, there], sems.at[2]),
        pltpu.make_async_copy(resid_buf, resid_ref.at[:, :, there], sems.at[3]),
    ]
    copies[0].start()
    copies[1].start()
    q_new = solve(total_ref, inverse_ref, groups)
    q_buf[...] = q_new
    copies[2].start()
    resid_buf[0] = residual(q_new, basis_ref, grads_ref[0, :, there])
    copies[3].start()
    for copy in copies:
        copy.wait()


def finish(sides, total, inverse, basis, grads, groups, done):
    rows, cols = grads.shape[1:]
    half = cols // NC
    return pl.pallas_call(
        functools.partial(finish_kernel, groups),
        in_specs=[pl.BlockSpec(memory_space=pltpu.SMEM)] + [pl.BlockSpec(memory_space=pltpu.VMEM)] * 6,
        out_specs=(pl.BlockSpec(memory_space=pl.ANY),) * 2,
        out_shape=(
            jax.ShapeDtypeStruct((RANK, cols), F32),
            jax.ShapeDtypeStruct((1, rows, cols), BF16),
        ),
        scratch_shapes=[
            pltpu.VMEM((RANK, half), F32),
            pltpu.VMEM((1, rows, half), BF16),
            pltpu.SemaphoreType.DMA((4,)),
        ],
        compiler_params=pltpu.CompilerParams(vmem_limit_bytes=VMEM),
        name="finish",
    )(sides, total, inverse, basis, grads, *done)


def exchange(blocks, axis):
    return lax.all_to_all(blocks, axis, 0, 0, tiled=True)


def spread(block, axis):
    return exchange(jnp.broadcast_to(block[None], (lax.axis_size(axis),) + block.shape), axis)


def per_device(grads, q_prev):
    groups = lax.axis_size(("far", "near"))
    swap = [(0, 1), (1, 0)]
    own = lax.axis_index("c").astype(jnp.int32).reshape(1)

    shares, grads, sides = project(own, grads, q_prev, groups)
    shares = exchange(shares, ("far", "near"))
    away = lax.ppermute(term(1, sides, shares, grads), "c", swap)
    part = term(0, sides, shares, grads) + away
    used = part.shape[1]
    part = jnp.sum(exchange(part, ("x", "near")), axis=0)
    part = jnp.pad(part, ((0, NY * TILES - used), (0, 0), (0, 0)))
    part = jnp.sum(exchange(part.reshape(NY, TILES, SUB, LANE), "y"), axis=0)
    part = jnp.sum(spread(part, "far"), axis=0)

    total = spread(part, "y").reshape(NY * TILES, SUB, LANE)[:used]
    total = spread(total, ("x", "near"))
    away = lax.ppermute(total, "c", swap)
    inverse, basis = factor(total[0, used - 1], shares, grads.shape[1])
    done = mine(sides, total, inverse, basis, grads, groups)
    return tuple(finish(sides, away, inverse, basis, grads, groups, done))


def solution(mesh):
    groups = mesh.devices.shape[1]
    fine = Mesh(mesh.devices.reshape(NY, NX, NC, groups // NP, NP), ("y", "x", "c", "far", "near"))
    split = P(("far", "near"), ("y", "x", "c"), None)
    return jax.shard_map(per_device, mesh=fine, in_specs=(split, P()), out_specs=(P(), split), check_vma=False)
```

```python
import functools

import jax
import jax.numpy as jnp
from jax import lax
from jax.experimental import pallas as pl
from jax.experimental.pallas import tpu as pltpu
from jax.sharding import Mesh, PartitionSpec as P

HIGH = lax.Precision.HIGHEST
F32, BF16 = jnp.float32, jnp.bfloat16
NY, NX, NC, PAIR = 4, 4, 2, 2
NP = PAIR * PAIR
SUB, LANE = 8, 128
RANK = 32
TILES = 4
COPIES = 2
AHEAD = 4
VMEM = 24 * 1024 * 1024


def pieces(value, count):
    parts = []
    for _ in range(count):
        part = value.astype(BF16)
        parts.append(part)
        value = value - part.astype(F32)
    return parts


def dot(a, b, contract, precision=None):
    dims = ((contract[0:1], contract[1:2]), ((), ()))
    return lax.dot_general(a, b, dims, precision=precision, preferred_element_type=F32)


def left_of(shares_ref):
    packed = shares_ref[0]
    for g in range(1, shares_ref.shape[0]):
        packed = packed + shares_ref[g]
    half = LANE // 2
    return jnp.concatenate([packed[:, :half], packed[:, half:]], axis=0)


def project_kernel(own_ref, grads_ref, q_ref, out_ref, grads_buf, sides_ref, q_buf, sems):
    sides_ref[0] = own_ref[0]
    sides_ref[1] = 1 - own_ref[0]
    count = sems.shape[0]
    wide = q_buf.shape[1] // count
    copies = []
    for n in range(count):
        cols = pl.ds(n * wide, wide)
        copies.append(
            (
                pltpu.make_async_copy(grads_ref.at[:, :, cols], grads_buf.at[:, :, cols], sems.at[n, 0]),
                pltpu.make_async_copy(q_ref.at[:, cols], q_buf.at[:, cols], sems.at[n, 1]),
            )
        )
        for copy in copies[-1]:
            copy.start()
    total = None
    for n in range(count):
        for copy in copies[n]:
            copy.wait()
        cols = pl.ds(n * wide, wide)
        stack = jnp.concatenate(pieces(q_buf[:, cols], 2), axis=0)
        part = dot(stack, grads_buf[0, :, cols], (1, 1))
        total = part if total is None else total + part
    local = total[:RANK] + total[RANK:]
    packed = jnp.concatenate([local[: RANK // 2], local[RANK // 2 :]], axis=1)
    for g in range(out_ref.shape[0]):
        out_ref[g] = packed


def project(own, grads, q_prev, groups):
    rows, cols = grads.shape[1:]
    return pl.pallas_call(
        project_kernel,
        in_specs=[pl.BlockSpec(memory_space=pltpu.SMEM)] + [pl.BlockSpec(memory_space=pl.ANY)] * 2,
        out_specs=(
            pl.BlockSpec(memory_space=pltpu.VMEM),
            pl.BlockSpec(memory_space=pltpu.VMEM),
            pl.BlockSpec(memory_space=pltpu.SMEM),
        ),
        out_shape=(
            jax.ShapeDtypeStruct((groups, RANK // 2, LANE), F32),
            pltpu.VMEM(grads.shape, BF16),
            jax.ShapeDtypeStruct((2,), jnp.int32),
        ),
        scratch_shapes=[
            pltpu.VMEM((RANK, cols), F32),
            pltpu.SemaphoreType.DMA((COPIES, 2)),
        ],
        compiler_params=pltpu.CompilerParams(vmem_limit_bytes=VMEM),
        name="project",
    )(own, pltpu.with_memory_space_constraint(grads, pltpu.HBM), pltpu.with_memory_space_constraint(q_prev, pltpu.HBM))


def term_kernel(side, sides_ref, shares_ref, grads_ref, out_ref):
    left = left_of(shares_ref)
    stack = jnp.concatenate(pieces(left, 2), axis=0)
    half = grads_ref.shape[2] // NC
    part = dot(stack, grads_ref[0, :, half_of(side, sides_ref, half)], (1, 0))
    part = part[:RANK] + part[RANK:]
    tiles = out_ref.shape[1] - 1
    wide = dot(left, jnp.concatenate([left] * NX, axis=0), (1, 1), HIGH) / shares_ref.shape[0]
    slot = lax.broadcasted_iota(jnp.int32, (SUB, LANE), 1) // RANK
    tile = jnp.zeros((SUB, LANE), F32)
    for x in range(NX):
        tile = jnp.where(slot == x, wide[x * SUB : (x + 1) * SUB], tile)
    for x in range(NX):
        for p in range(NP):
            for t in range(tiles):
                cols = slice((p * tiles + t) * LANE, (p * tiles + t + 1) * LANE)
                out_ref[x * NP + p, t] = part[x * SUB : (x + 1) * SUB, cols]
            out_ref[x * NP + p, tiles] = tile


def term(side, sides, shares, grads):
    rows, cols = grads.shape[1:]
    half = cols // NC
    shape = (NX * NP, half // NP // LANE + 1, SUB, LANE)
    return pl.pallas_call(
        functools.partial(term_kernel, side),
        in_specs=[pl.BlockSpec(memory_space=pltpu.SMEM)] + [pl.BlockSpec(memory_space=pltpu.VMEM)] * 2,
        out_specs=pl.BlockSpec(memory_space=pltpu.VMEM),
        out_shape=jax.ShapeDtypeStruct(shape, F32),
        compiler_params=pltpu.CompilerParams(vmem_limit_bytes=VMEM),
        cost_estimate=pl.CostEstimate(flops=2 * 96 * rows * half, bytes_accessed=6 * rows * half, transcendentals=0),
        name="term",
    )(sides, shares, grads)


def factor_kernel(gram_ref, shares_ref, inverse_ref, basis_ref):
    tile = gram_ref[...]
    lane = lax.broadcasted_iota(jnp.int32, (RANK, LANE), 1)
    row = lax.broadcasted_iota(jnp.int32, (RANK, LANE), 0)
    work = jnp.concatenate([pltpu.roll(tile, (LANE - RANK * x) % LANE, 1) for x in range(NX)], axis=0)
    work = jnp.where(lane < RANK, work, jnp.where(lane - RANK == row, 1.0, 0.0))
    for k in range(0, RANK, AHEAD):
        downs = [jnp.broadcast_to(work[:, j : j + 1], work.shape) for j in range(k, k + AHEAD)]
        rights = [work[j : j + 1] for j in range(k, k + AHEAD)]
        for j in range(AHEAD):
            down = downs[j]
            scale = 1.0 / down[k + j : k + j + 1]
            across = rights[j] * scale
            for i in range(j + 1, AHEAD):
                ratio = down[k + i : k + i + 1]
                rights[i] = rights[i] - ratio * across
                downs[i] = downs[i] - down * (ratio * scale)
            work = jnp.where(row > k + j, work - down * across, work)
    pivots = jnp.sum(jnp.where(lane == row, work, 0.0), axis=1, keepdims=True)
    work = work * (1.0 / jnp.sqrt(pivots))
    inverse = jnp.where(lane < RANK, pltpu.roll(work, LANE - RANK, 1), 0.0)
    one, two = [part.astype(F32) for part in pieces(inverse, 2)]
    one = one + pltpu.roll(one, RANK, 1)
    two = two + pltpu.roll(two, RANK, 1)
    inverse_ref[...] = (one + pltpu.roll(two, 2 * RANK, 1)).astype(BF16)
    basis = dot(left_of(shares_ref), jnp.concatenate([inverse[:, :RANK]] * 4, axis=0), (0, 1), HIGH)
    high = basis.astype(BF16).astype(F32)
    wide = lax.broadcasted_iota(jnp.int32, basis.shape, 1)
    basis_ref[...] = jnp.where(wide < LANE // 2, high, basis - high).astype(BF16)


def factor(gram, shares, rows):
    return pl.pallas_call(
        factor_kernel,
        out_shape=(
            jax.ShapeDtypeStruct((RANK, LANE), BF16),
            jax.ShapeDtypeStruct((rows, LANE), BF16),
        ),
        compiler_params=pltpu.CompilerParams(vmem_limit_bytes=VMEM),
        cost_estimate=pl.CostEstimate(flops=1 << 22, bytes_accessed=1 << 20, transcendentals=32),
        name="factor",
    )(gram, shares)


def solve(total_ref, inverse_ref, groups):
    tiles = total_ref.shape[1] - 1
    columns = []
    for t in range(NP * tiles):
        parts = [total_ref[x * NP + t // tiles, t % tiles] for x in range(NX)]
        columns.append(jnp.concatenate(parts, axis=0))
    one, two = pieces(jnp.concatenate(columns, axis=1), 2)
    return dot(inverse_ref[...], jnp.concatenate([one, two, one, two], axis=0), (1, 0)) / groups


def residual(q_new, basis_ref, grads):
    high, low = pieces(q_new, 2)
    approx = dot(basis_ref[...], jnp.concatenate([high, low, high, low], axis=0), (1, 0))
    return (grads.astype(F32) - approx).astype(BF16)


def half_of(side, sides_ref, half):
    return pl.ds(pl.multiple_of(sides_ref[side] * half, LANE), half)


def mine_kernel(groups, sides_ref, total_ref, inverse_ref, basis_ref, grads_ref, q_ref, resid_ref):
    q_new = solve(total_ref, inverse_ref, groups)
    q_ref[...] = q_new
    resid_ref[0] = residual(q_new, basis_ref, grads_ref[0, :, half_of(0, sides_ref, q_ref.shape[1])])


def mine(sides, total, inverse, basis, grads, groups):
    rows, cols = grads.shape[1:]
    half = cols // NC
    return pl.pallas_call(
        functools.partial(mine_kernel, groups),
        in_specs=[pl.BlockSpec(memory_space=pltpu.SMEM)] + [pl.BlockSpec(memory_space=pltpu.VMEM)] * 4,
        out_specs=(pl.BlockSpec(memory_space=pltpu.VMEM),) * 2,
        out_shape=(pltpu.VMEM((RANK, half), F32), pltpu.VMEM((1, rows, half), BF16)),
        compiler_params=pltpu.CompilerParams(vmem_limit_bytes=VMEM),
        cost_estimate=pl.CostEstimate(flops=2 * 160 * rows * half, bytes_accessed=6 * rows * half, transcendentals=0),
        name="mine",
    )(sides, total, inverse, basis, grads)


def finish_kernel(
    groups, sides_ref, total_ref, inverse_ref, basis_ref, grads_ref, mine_q_ref, mine_resid_ref,
    q_ref, resid_ref, q_buf, resid_buf, sems,
):
    half = q_buf.shape[1]
    here, there = half_of(0, sides_ref, half), half_of(1, sides_ref, half)
    copies = [
        pltpu.make_async_copy(mine_q_ref, q_ref.at[:, here], sems.at[0]),
        pltpu.make_async_copy(mine_resid_ref, resid_ref.at[:, :, here], sems.at[1]),
        pltpu.make_async_copy(q_buf, q_ref.at[:, there], sems.at[2]),
        pltpu.make_async_copy(resid_buf, resid_ref.at[:, :, there], sems.at[3]),
    ]
    copies[0].start()
    copies[1].start()
    q_new = solve(total_ref, inverse_ref, groups)
    q_buf[...] = q_new
    copies[2].start()
    resid_buf[0] = residual(q_new, basis_ref, grads_ref[0, :, there])
    copies[3].start()
    for copy in copies:
        copy.wait()


def finish(sides, total, inverse, basis, grads, groups, done):
    rows, cols = grads.shape[1:]
    half = cols // NC
    return pl.pallas_call(
        functools.partial(finish_kernel, groups),
        in_specs=[pl.BlockSpec(memory_space=pltpu.SMEM)] + [pl.BlockSpec(memory_space=pltpu.VMEM)] * 6,
        out_specs=(pl.BlockSpec(memory_space=pl.ANY),) * 2,
        out_shape=(
            jax.ShapeDtypeStruct((RANK, cols), F32),
            jax.ShapeDtypeStruct((1, rows, cols), BF16),
        ),
        scratch_shapes=[
            pltpu.VMEM((RANK, half), F32),
            pltpu.VMEM((1, rows, half), BF16),
            pltpu.SemaphoreType.DMA((4,)),
        ],
        compiler_params=pltpu.CompilerParams(vmem_limit_bytes=VMEM),
        name="finish",
    )(sides, total, inverse, basis, grads, *done)


def exchange(blocks, axis):
    return lax.all_to_all(blocks, axis, 0, 0, tiled=True)


def spread(block, axis):
    return exchange(jnp.broadcast_to(block[None], (lax.axis_size(axis),) + block.shape), axis)


def per_device(grads, q_prev):
    groups = lax.axis_size(("far", "near"))
    swap = [(0, 1), (1, 0)]
    own = lax.axis_index("c").astype(jnp.int32).reshape(1)

    shares, grads, sides = project(own, grads, q_prev, groups)
    shares = exchange(shares, ("far", "near"))
    away = lax.ppermute(term(1, sides, shares, grads), "c", swap)
    part = term(0, sides, shares, grads) + away
    used = part.shape[1]
    part = jnp.sum(exchange(part, ("x", "near", "side")), axis=0)
    part = jnp.pad(part, ((0, NY * TILES - used), (0, 0), (0, 0)))
    part = jnp.sum(exchange(part.reshape(NY, TILES, SUB, LANE), "y"), axis=0)
    part = jnp.sum(spread(part, "far"), axis=0)

    total = spread(part, "y").reshape(NY * TILES, SUB, LANE)[:used]
    total = spread(total, ("x", "near", "side"))
    away = lax.ppermute(total, "c", swap)
    inverse, basis = factor(total[0, used - 1], shares, grads.shape[1])
    done = mine(sides, total, inverse, basis, grads, groups)
    return tuple(finish(sides, away, inverse, basis, grads, groups, done))


def solution(mesh):
    groups = mesh.devices.shape[1]
    shape = (NY, PAIR, NX, NC, groups // PAIR, PAIR)
    fine = Mesh(mesh.devices.reshape(shape), ("y", "side", "x", "c", "far", "near"))
    split = P(("far", "near"), ("y", "side", "x", "c"), None)
    return jax.shard_map(per_device, mesh=fine, in_specs=(split, P()), out_specs=(P(), split), check_vma=False)
```

```python
import functools

import jax
import jax.numpy as jnp
from jax import lax
from jax.experimental import pallas as pl
from jax.experimental.pallas import tpu as pltpu
from jax.sharding import Mesh, PartitionSpec as P

HIGH = lax.Precision.HIGHEST
F32, BF16 = jnp.float32, jnp.bfloat16
NY, NX, NC, PAIR = 4, 4, 2, 2
NP = PAIR * PAIR
SUB, LANE = 8, 128
RANK = 32
COPIES = 2
AHEAD = 4
VMEM = 24 * 1024 * 1024


def pieces(value, count):
    parts = []
    for _ in range(count):
        part = value.astype(BF16)
        parts.append(part)
        value = value - part.astype(F32)
    return parts


def dot(a, b, contract, precision=None):
    dims = ((contract[0:1], contract[1:2]), ((), ()))
    return lax.dot_general(a, b, dims, precision=precision, preferred_element_type=F32)


def left_of(shares_ref):
    packed = shares_ref[0]
    for g in range(1, shares_ref.shape[0]):
        packed = packed + shares_ref[g]
    half = LANE // 2
    return jnp.concatenate([packed[:, :half], packed[:, half:]], axis=0)


def project_kernel(own_ref, grads_ref, q_ref, out_ref, grads_buf, sides_ref, q_buf, sems):
    sides_ref[0] = own_ref[0]
    sides_ref[1] = 1 - own_ref[0]
    count = sems.shape[0]
    wide = q_buf.shape[1] // count
    copies = []
    for n in range(count):
        cols = pl.ds(n * wide, wide)
        copies.append(
            (
                pltpu.make_async_copy(grads_ref.at[:, :, cols], grads_buf.at[:, :, cols], sems.at[n, 0]),
                pltpu.make_async_copy(q_ref.at[:, cols], q_buf.at[:, cols], sems.at[n, 1]),
            )
        )
        for copy in copies[-1]:
            copy.start()
    total = None
    for n in range(count):
        for copy in copies[n]:
            copy.wait()
        cols = pl.ds(n * wide, wide)
        stack = jnp.concatenate(pieces(q_buf[:, cols], 2), axis=0)
        part = dot(stack, grads_buf[0, :, cols], (1, 1))
        total = part if total is None else total + part
    local = total[:RANK] + total[RANK:]
    packed = jnp.concatenate([local[: RANK // 2], local[RANK // 2 :]], axis=1)
    for g in range(out_ref.shape[0]):
        out_ref[g] = packed


def project(own, grads, q_prev, groups):
    rows, cols = grads.shape[1:]
    return pl.pallas_call(
        project_kernel,
        in_specs=[pl.BlockSpec(memory_space=pltpu.SMEM)] + [pl.BlockSpec(memory_space=pl.ANY)] * 2,
        out_specs=(
            pl.BlockSpec(memory_space=pltpu.VMEM),
            pl.BlockSpec(memory_space=pltpu.VMEM),
            pl.BlockSpec(memory_space=pltpu.SMEM),
        ),
        out_shape=(
            jax.ShapeDtypeStruct((groups, RANK // 2, LANE), F32),
            pltpu.VMEM(grads.shape, BF16),
            jax.ShapeDtypeStruct((2,), jnp.int32),
        ),
        scratch_shapes=[
            pltpu.VMEM((RANK, cols), F32),
            pltpu.SemaphoreType.DMA((COPIES, 2)),
        ],
        compiler_params=pltpu.CompilerParams(vmem_limit_bytes=VMEM),
        name="project",
    )(own, pltpu.with_memory_space_constraint(grads, pltpu.HBM), pltpu.with_memory_space_constraint(q_prev, pltpu.HBM))


def term_kernel(side, sides_ref, shares_ref, grads_ref, out_ref):
    left = left_of(shares_ref)
    stack = jnp.concatenate(pieces(left, 2), axis=0)
    half = grads_ref.shape[2] // NC
    part = dot(stack, grads_ref[0, :, half_of(side, sides_ref, half)], (1, 0))
    part = part[:RANK] + part[RANK:]
    tiles = out_ref.shape[1] - 1
    wide = dot(left, jnp.concatenate([left] * NX, axis=0), (1, 1), HIGH) / shares_ref.shape[0]
    slot = lax.broadcasted_iota(jnp.int32, (SUB, LANE), 1) // RANK
    tile = jnp.zeros((SUB, LANE), F32)
    for x in range(NX):
        tile = jnp.where(slot == x, wide[x * SUB : (x + 1) * SUB], tile)
    for x in range(NX):
        for p in range(NP):
            for t in range(tiles):
                cols = slice((p * tiles + t) * LANE, (p * tiles + t + 1) * LANE)
                out_ref[x * NP + p, t] = part[x * SUB : (x + 1) * SUB, cols]
            out_ref[x * NP + p, tiles] = tile


def term(side, sides, shares, grads):
    rows, cols = grads.shape[1:]
    half = cols // NC
    shape = (NX * NP, half // NP // LANE + 1, SUB, LANE)
    return pl.pallas_call(
        functools.partial(term_kernel, side),
        in_specs=[pl.BlockSpec(memory_space=pltpu.SMEM)] + [pl.BlockSpec(memory_space=pltpu.VMEM)] * 2,
        out_specs=pl.BlockSpec(memory_space=pltpu.VMEM),
        out_shape=jax.ShapeDtypeStruct(shape, F32),
        compiler_params=pltpu.CompilerParams(vmem_limit_bytes=VMEM),
        cost_estimate=pl.CostEstimate(flops=2 * 96 * rows * half, bytes_accessed=6 * rows * half, transcendentals=0),
        name="term",
    )(sides, shares, grads)


def factor_kernel(gram_ref, shares_ref, inverse_ref, basis_ref):
    tile = gram_ref[...]
    lane = lax.broadcasted_iota(jnp.int32, (RANK, LANE), 1)
    row = lax.broadcasted_iota(jnp.int32, (RANK, LANE), 0)
    work = jnp.concatenate([pltpu.roll(tile, (LANE - RANK * x) % LANE, 1) for x in range(NX)], axis=0)
    work = jnp.where(lane < RANK, work, jnp.where(lane - RANK == row, 1.0, 0.0))
    for k in range(0, RANK, AHEAD):
        downs = [jnp.broadcast_to(work[:, j : j + 1], work.shape) for j in range(k, k + AHEAD)]
        rights = [work[j : j + 1] for j in range(k, k + AHEAD)]
        for j in range(AHEAD):
            down = downs[j]
            scale = 1.0 / down[k + j : k + j + 1]
            across = rights[j] * scale
            for i in range(j + 1, AHEAD):
                ratio = down[k + i : k + i + 1]
                rights[i] = rights[i] - ratio * across
                downs[i] = downs[i] - down * (ratio * scale)
            work = jnp.where(row > k + j, work - down * across, work)
    pivots = jnp.sum(jnp.where(lane == row, work, 0.0), axis=1, keepdims=True)
    work = work * (1.0 / jnp.sqrt(pivots))
    inverse = jnp.where(lane < RANK, pltpu.roll(work, LANE - RANK, 1), 0.0)
    one, two = [part.astype(F32) for part in pieces(inverse, 2)]
    one = one + pltpu.roll(one, RANK, 1)
    two = two + pltpu.roll(two, RANK, 1)
    inverse_ref[...] = (one + pltpu.roll(two, 2 * RANK, 1)).astype(BF16)
    basis = dot(left_of(shares_ref), jnp.concatenate([inverse[:, :RANK]] * 4, axis=0), (0, 1), HIGH)
    high = basis.astype(BF16).astype(F32)
    wide = lax.broadcasted_iota(jnp.int32, basis.shape, 1)
    basis_ref[...] = jnp.where(wide < LANE // 2, high, basis - high).astype(BF16)


def factor(gram, shares, rows):
    return pl.pallas_call(
        factor_kernel,
        out_shape=(
            jax.ShapeDtypeStruct((RANK, LANE), BF16),
            jax.ShapeDtypeStruct((rows, LANE), BF16),
        ),
        compiler_params=pltpu.CompilerParams(vmem_limit_bytes=VMEM),
        cost_estimate=pl.CostEstimate(flops=1 << 22, bytes_accessed=1 << 20, transcendentals=32),
        name="factor",
    )(gram, shares)


def solve(total_ref, inverse_ref, groups):
    tiles = total_ref.shape[1] - 1
    columns = []
    for t in range(NP * tiles):
        parts = [total_ref[x * NP + t // tiles, t % tiles] for x in range(NX)]
        columns.append(jnp.concatenate(parts, axis=0))
    one, two = pieces(jnp.concatenate(columns, axis=1), 2)
    return dot(inverse_ref[...], jnp.concatenate([one, two, one, two], axis=0), (1, 0)) / groups


def residual(q_new, basis_ref, grads):
    high, low = pieces(q_new, 2)
    approx = dot(basis_ref[...], jnp.concatenate([high, low, high, low], axis=0), (1, 0))
    return (grads.astype(F32) - approx).astype(BF16)


def half_of(side, sides_ref, half):
    return pl.ds(pl.multiple_of(sides_ref[side] * half, LANE), half)


def mine_kernel(groups, sides_ref, total_ref, inverse_ref, basis_ref, grads_ref, q_ref, resid_ref):
    q_new = solve(total_ref, inverse_ref, groups)
    q_ref[...] = q_new
    resid_ref[0] = residual(q_new, basis_ref, grads_ref[0, :, half_of(0, sides_ref, q_ref.shape[1])])


def mine(sides, total, inverse, basis, grads, groups):
    rows, cols = grads.shape[1:]
    half = cols // NC
    return pl.pallas_call(
        functools.partial(mine_kernel, groups),
        in_specs=[pl.BlockSpec(memory_space=pltpu.SMEM)] + [pl.BlockSpec(memory_space=pltpu.VMEM)] * 4,
        out_specs=(pl.BlockSpec(memory_space=pltpu.VMEM),) * 2,
        out_shape=(pltpu.VMEM((RANK, half), F32), pltpu.VMEM((1, rows, half), BF16)),
        compiler_params=pltpu.CompilerParams(vmem_limit_bytes=VMEM),
        cost_estimate=pl.CostEstimate(flops=2 * 160 * rows * half, bytes_accessed=6 * rows * half, transcendentals=0),
        name="mine",
    )(sides, total, inverse, basis, grads)


def finish_kernel(
    groups, sides_ref, total_ref, inverse_ref, basis_ref, grads_ref, mine_q_ref, mine_resid_ref,
    q_ref, resid_ref, q_buf, resid_buf, sems,
):
    half = q_buf.shape[1]
    here, there = half_of(0, sides_ref, half), half_of(1, sides_ref, half)
    copies = [
        pltpu.make_async_copy(mine_q_ref, q_ref.at[:, here], sems.at[0]),
        pltpu.make_async_copy(mine_resid_ref, resid_ref.at[:, :, here], sems.at[1]),
        pltpu.make_async_copy(q_buf, q_ref.at[:, there], sems.at[2]),
        pltpu.make_async_copy(resid_buf, resid_ref.at[:, :, there], sems.at[3]),
    ]
    copies[0].start()
    copies[1].start()
    q_new = solve(total_ref, inverse_ref, groups)
    q_buf[...] = q_new
    copies[2].start()
    resid_buf[0] = residual(q_new, basis_ref, grads_ref[0, :, there])
    copies[3].start()
    for copy in copies:
        copy.wait()


def finish(sides, total, inverse, basis, grads, groups, done):
    rows, cols = grads.shape[1:]
    half = cols // NC
    return pl.pallas_call(
        functools.partial(finish_kernel, groups),
        in_specs=[pl.BlockSpec(memory_space=pltpu.SMEM)] + [pl.BlockSpec(memory_space=pltpu.VMEM)] * 6,
        out_specs=(pl.BlockSpec(memory_space=pl.ANY),) * 2,
        out_shape=(
            jax.ShapeDtypeStruct((RANK, cols), F32),
            jax.ShapeDtypeStruct((1, rows, cols), BF16),
        ),
        scratch_shapes=[
            pltpu.VMEM((RANK, half), F32),
            pltpu.VMEM((1, rows, half), BF16),
            pltpu.SemaphoreType.DMA((4,)),
        ],
        compiler_params=pltpu.CompilerParams(vmem_limit_bytes=VMEM),
        name="finish",
    )(sides, total, inverse, basis, grads, *done)


def exchange(blocks, axis):
    return lax.all_to_all(blocks, axis, 0, 0, tiled=True)


def spread(block, axis):
    return exchange(jnp.broadcast_to(block[None], (lax.axis_size(axis),) + block.shape), axis)


def per_device(grads, q_prev):
    groups = lax.axis_size(("far", "near"))
    swap = [(0, 1), (1, 0)]
    own = lax.axis_index("c").astype(jnp.int32).reshape(1)

    shares, grads, sides = project(own, grads, q_prev, groups)
    shares = exchange(shares, ("far", "near"))
    away = lax.ppermute(term(1, sides, shares, grads), "c", swap)
    part = term(0, sides, shares, grads) + away
    used = part.shape[1]
    part = jnp.sum(exchange(part, ("x", "near", "side")), axis=0)
    part = jnp.sum(spread(part, "y"), axis=0)
    part = jnp.sum(spread(part, "far"), axis=0)
    total = spread(part, ("x", "near", "side"))
    away = lax.ppermute(total, "c", swap)
    inverse, basis = factor(total[0, used - 1], shares, grads.shape[1])
    done = mine(sides, total, inverse, basis, grads, groups)
    return tuple(finish(sides, away, inverse, basis, grads, groups, done))


def solution(mesh):
    groups = mesh.devices.shape[1]
    shape = (NY, PAIR, NX, NC, groups // PAIR, PAIR)
    fine = Mesh(mesh.devices.reshape(shape), ("y", "side", "x", "c", "far", "near"))
    split = P(("far", "near"), ("y", "side", "x", "c"), None)
    return jax.shard_map(per_device, mesh=fine, in_specs=(split, P()), out_specs=(P(), split), check_vma=False)
```

```python
import functools

import jax
import jax.numpy as jnp
from jax import lax
from jax.experimental import pallas as pl
from jax.experimental.pallas import tpu as pltpu
from jax.sharding import Mesh, PartitionSpec as P

HIGH = lax.Precision.HIGHEST
F32, BF16 = jnp.float32, jnp.bfloat16
NY, NX, NC, PAIR = 4, 4, 2, 2
NP = PAIR * PAIR
SUB, LANE = 8, 128
RANK = 32
COPIES = 2
AHEAD = 4
VMEM = 24 * 1024 * 1024


def pieces(value, count):
    parts = []
    for _ in range(count):
        part = value.astype(BF16)
        parts.append(part)
        value = value - part.astype(F32)
    return parts


def dot(a, b, contract, precision=None):
    dims = ((contract[0:1], contract[1:2]), ((), ()))
    return lax.dot_general(a, b, dims, precision=precision, preferred_element_type=F32)


def left_of(shares_ref):
    packed = shares_ref[0]
    for g in range(1, shares_ref.shape[0]):
        packed = packed + shares_ref[g]
    half = LANE // 2
    return jnp.concatenate([packed[:, :half], packed[:, half:]], axis=0)


def project_kernel(own_ref, grads_ref, q_ref, out_ref, grads_buf, sides_ref, q_buf, sems):
    sides_ref[0] = own_ref[0]
    sides_ref[1] = 1 - own_ref[0]
    count = sems.shape[0]
    wide = q_buf.shape[1] // count
    copies = []
    for n in range(count):
        cols = pl.ds(n * wide, wide)
        copies.append(
            (
                pltpu.make_async_copy(grads_ref.at[:, :, cols], grads_buf.at[:, :, cols], sems.at[n, 0]),
                pltpu.make_async_copy(q_ref.at[:, cols], q_buf.at[:, cols], sems.at[n, 1]),
            )
        )
        for copy in copies[-1]:
            copy.start()
    total = None
    for n in range(count):
        for copy in copies[n]:
            copy.wait()
        cols = pl.ds(n * wide, wide)
        stack = jnp.concatenate(pieces(q_buf[:, cols], 2), axis=0)
        part = dot(stack, grads_buf[0, :, cols], (1, 1))
        total = part if total is None else total + part
    local = total[:RANK] + total[RANK:]
    packed = jnp.concatenate([local[: RANK // 2], local[RANK // 2 :]], axis=1)
    for g in range(out_ref.shape[0]):
        out_ref[g] = packed


def project(own, grads, q_prev, groups):
    rows, cols = grads.shape[1:]
    return pl.pallas_call(
        project_kernel,
        in_specs=[pl.BlockSpec(memory_space=pltpu.SMEM)] + [pl.BlockSpec(memory_space=pl.ANY)] * 2,
        out_specs=(
            pl.BlockSpec(memory_space=pltpu.VMEM),
            pl.BlockSpec(memory_space=pltpu.VMEM),
            pl.BlockSpec(memory_space=pltpu.SMEM),
        ),
        out_shape=(
            jax.ShapeDtypeStruct((groups, RANK // 2, LANE), F32),
            pltpu.VMEM(grads.shape, BF16),
            jax.ShapeDtypeStruct((2,), jnp.int32),
        ),
        scratch_shapes=[
            pltpu.VMEM((RANK, cols), F32),
            pltpu.SemaphoreType.DMA((COPIES, 2)),
        ],
        compiler_params=pltpu.CompilerParams(vmem_limit_bytes=VMEM),
        name="project",
    )(own, pltpu.with_memory_space_constraint(grads, pltpu.HBM), pltpu.with_memory_space_constraint(q_prev, pltpu.HBM))


def term_kernel(side, sides_ref, shares_ref, grads_ref, out_ref):
    left = left_of(shares_ref)
    stack = jnp.concatenate(pieces(left, 2), axis=0)
    half = grads_ref.shape[2] // NC
    part = dot(stack, grads_ref[0, :, half_of(side, sides_ref, half)], (1, 0))
    part = part[:RANK] + part[RANK:]
    tiles = out_ref.shape[1] - 1
    wide = dot(left, jnp.concatenate([left] * NX, axis=0), (1, 1), HIGH) / PAIR
    slot = lax.broadcasted_iota(jnp.int32, (SUB, LANE), 1) // RANK
    tile = jnp.zeros((SUB, LANE), F32)
    for x in range(NX):
        tile = jnp.where(slot == x, wide[x * SUB : (x + 1) * SUB], tile)
    for x in range(NX):
        for p in range(NP):
            for t in range(tiles):
                cols = slice((p * tiles + t) * LANE, (p * tiles + t + 1) * LANE)
                out_ref[x * NP + p, t] = part[x * SUB : (x + 1) * SUB, cols]
            out_ref[x * NP + p, tiles] = tile


def term(side, sides, shares, grads):
    rows, cols = grads.shape[1:]
    half = cols // NC
    shape = (NX * NP, half // NP // LANE + 1, SUB, LANE)
    return pl.pallas_call(
        functools.partial(term_kernel, side),
        in_specs=[pl.BlockSpec(memory_space=pltpu.SMEM)] + [pl.BlockSpec(memory_space=pltpu.VMEM)] * 2,
        out_specs=pl.BlockSpec(memory_space=pltpu.VMEM),
        out_shape=jax.ShapeDtypeStruct(shape, F32),
        compiler_params=pltpu.CompilerParams(vmem_limit_bytes=VMEM),
        cost_estimate=pl.CostEstimate(flops=2 * 96 * rows * half, bytes_accessed=6 * rows * half, transcendentals=0),
        name="term",
    )(sides, shares, grads)


def factor_kernel(gram_ref, shares_ref, inverse_ref, basis_ref):
    tile = gram_ref[...]
    lane = lax.broadcasted_iota(jnp.int32, (RANK, LANE), 1)
    row = lax.broadcasted_iota(jnp.int32, (RANK, LANE), 0)
    work = jnp.concatenate([pltpu.roll(tile, (LANE - RANK * x) % LANE, 1) for x in range(NX)], axis=0)
    work = jnp.where(lane < RANK, work, jnp.where(lane - RANK == row, 1.0, 0.0))
    for k in range(0, RANK, AHEAD):
        downs = [jnp.broadcast_to(work[:, j : j + 1], work.shape) for j in range(k, k + AHEAD)]
        rights = [work[j : j + 1] for j in range(k, k + AHEAD)]
        for j in range(AHEAD):
            down = downs[j]
            scale = 1.0 / down[k + j : k + j + 1]
            across = rights[j] * scale
            for i in range(j + 1, AHEAD):
                ratio = down[k + i : k + i + 1]
                rights[i] = rights[i] - ratio * across
                downs[i] = downs[i] - down * (ratio * scale)
            work = jnp.where(row > k + j, work - down * across, work)
    pivots = jnp.sum(jnp.where(lane == row, work, 0.0), axis=1, keepdims=True)
    work = work * (1.0 / jnp.sqrt(pivots))
    inverse = jnp.where(lane < RANK, pltpu.roll(work, LANE - RANK, 1), 0.0)
    one, two = [part.astype(F32) for part in pieces(inverse, 2)]
    one = one + pltpu.roll(one, RANK, 1)
    two = two + pltpu.roll(two, RANK, 1)
    inverse_ref[...] = (one + pltpu.roll(two, 2 * RANK, 1)).astype(BF16)
    basis = dot(left_of(shares_ref), jnp.concatenate([inverse[:, :RANK]] * 4, axis=0), (0, 1), HIGH)
    high = basis.astype(BF16).astype(F32)
    wide = lax.broadcasted_iota(jnp.int32, basis.shape, 1)
    basis_ref[...] = jnp.where(wide < LANE // 2, high, basis - high).astype(BF16)


def factor(gram, shares, rows):
    return pl.pallas_call(
        factor_kernel,
        out_shape=(
            jax.ShapeDtypeStruct((RANK, LANE), BF16),
            jax.ShapeDtypeStruct((rows, LANE), BF16),
        ),
        compiler_params=pltpu.CompilerParams(vmem_limit_bytes=VMEM),
        cost_estimate=pl.CostEstimate(flops=1 << 22, bytes_accessed=1 << 20, transcendentals=32),
        name="factor",
    )(gram, shares)


def solve(total_ref, inverse_ref, groups):
    tiles = total_ref.shape[1]
    columns = []
    for t in range(NP * tiles):
        parts = [total_ref[x * NP + t // tiles, t % tiles] for x in range(NX)]
        columns.append(jnp.concatenate(parts, axis=0))
    one, two = pieces(jnp.concatenate(columns, axis=1), 2)
    return dot(inverse_ref[...], jnp.concatenate([one, two, one, two], axis=0), (1, 0)) / groups


def residual(q_new, basis_ref, grads):
    high, low = pieces(q_new, 2)
    approx = dot(basis_ref[...], jnp.concatenate([high, low, high, low], axis=0), (1, 0))
    return (grads.astype(F32) - approx).astype(BF16)


def half_of(side, sides_ref, half):
    return pl.ds(pl.multiple_of(sides_ref[side] * half, LANE), half)


def mine_kernel(groups, sides_ref, total_ref, inverse_ref, basis_ref, grads_ref, q_ref, resid_ref):
    q_new = solve(total_ref, inverse_ref, groups)
    q_ref[...] = q_new
    resid_ref[0] = residual(q_new, basis_ref, grads_ref[0, :, half_of(0, sides_ref, q_ref.shape[1])])


def mine(sides, total, inverse, basis, grads, groups):
    rows, cols = grads.shape[1:]
    half = cols // NC
    return pl.pallas_call(
        functools.partial(mine_kernel, groups),
        in_specs=[pl.BlockSpec(memory_space=pltpu.SMEM)] + [pl.BlockSpec(memory_space=pltpu.VMEM)] * 4,
        out_specs=(pl.BlockSpec(memory_space=pltpu.VMEM),) * 2,
        out_shape=(pltpu.VMEM((RANK, half), F32), pltpu.VMEM((1, rows, half), BF16)),
        compiler_params=pltpu.CompilerParams(vmem_limit_bytes=VMEM),
        cost_estimate=pl.CostEstimate(flops=2 * 160 * rows * half, bytes_accessed=6 * rows * half, transcendentals=0),
        name="mine",
    )(sides, total, inverse, basis, grads)


def finish_kernel(
    groups, sides_ref, total_ref, inverse_ref, basis_ref, grads_ref, mine_q_ref, mine_resid_ref,
    q_ref, resid_ref, q_buf, resid_buf, sems,
):
    half = q_buf.shape[1]
    here, there = half_of(0, sides_ref, half), half_of(1, sides_ref, half)
    copies = [
        pltpu.make_async_copy(mine_q_ref, q_ref.at[:, here], sems.at[0]),
        pltpu.make_async_copy(mine_resid_ref, resid_ref.at[:, :, here], sems.at[1]),
        pltpu.make_async_copy(q_buf, q_ref.at[:, there], sems.at[2]),
        pltpu.make_async_copy(resid_buf, resid_ref.at[:, :, there], sems.at[3]),
    ]
    copies[0].start()
    copies[1].start()
    q_new = solve(total_ref, inverse_ref, groups)
    q_buf[...] = q_new
    copies[2].start()
    resid_buf[0] = residual(q_new, basis_ref, grads_ref[0, :, there])
    copies[3].start()
    for copy in copies:
        copy.wait()


def finish(sides, total, inverse, basis, grads, groups, done):
    rows, cols = grads.shape[1:]
    half = cols // NC
    return pl.pallas_call(
        functools.partial(finish_kernel, groups),
        in_specs=[pl.BlockSpec(memory_space=pltpu.SMEM)] + [pl.BlockSpec(memory_space=pltpu.VMEM)] * 6,
        out_specs=(pl.BlockSpec(memory_space=pl.ANY),) * 2,
        out_shape=(
            jax.ShapeDtypeStruct((RANK, cols), F32),
            jax.ShapeDtypeStruct((1, rows, cols), BF16),
        ),
        scratch_shapes=[
            pltpu.VMEM((RANK, half), F32),
            pltpu.VMEM((1, rows, half), BF16),
            pltpu.SemaphoreType.DMA((4,)),
        ],
        compiler_params=pltpu.CompilerParams(vmem_limit_bytes=VMEM),
        name="finish",
    )(sides, total, inverse, basis, grads, *done)


def exchange(blocks, axis):
    return lax.all_to_all(blocks, axis, 0, 0, tiled=True)


def spread(block, axis):
    return exchange(jnp.broadcast_to(block[None], (lax.axis_size(axis),) + block.shape), axis)


def per_device(grads, q_prev):
    groups = lax.axis_size(("far", "near"))
    swap = [(0, 1), (1, 0)]
    own = lax.axis_index("c").astype(jnp.int32).reshape(1)

    shares, grads, sides = project(own, grads, q_prev, groups)
    shares = exchange(shares, ("far", "near"))
    away = lax.ppermute(term(1, sides, shares, grads), "c", swap)
    part = term(0, sides, shares, grads) + away
    part = jnp.sum(exchange(part, ("x", "near", "side")), axis=0)
    part = jnp.sum(spread(part, "y"), axis=0)
    gram = part[-1]
    part = jnp.sum(spread(part[:-1], "far"), axis=0)
    total = spread(part, ("x", "near", "side"))
    away = lax.ppermute(total, "c", swap)
    inverse, basis = factor(gram, shares, grads.shape[1])
    done = mine(sides, total, inverse, basis, grads, groups)
    return tuple(finish(sides, away, inverse, basis, grads, groups, done))


def solution(mesh):
    groups = mesh.devices.shape[1]
    shape = (NY, PAIR, NX, NC, groups // PAIR, PAIR)
    fine = Mesh(mesh.devices.reshape(shape), ("y", "side", "x", "c", "far", "near"))
    split = P(("far", "near"), ("y", "side", "x", "c"), None)
    return jax.shard_map(per_device, mesh=fine, in_specs=(split, P()), out_specs=(P(), split), check_vma=False)
```

```python
import functools

import jax
import jax.numpy as jnp
from jax import lax
from jax.experimental import pallas as pl
from jax.experimental.pallas import tpu as pltpu
from jax.sharding import Mesh, PartitionSpec as P

HIGH = lax.Precision.HIGHEST
F32, BF16 = jnp.float32, jnp.bfloat16
NY, NX, NC, PAIR = 4, 4, 2, 2
NP = PAIR * PAIR
SUB, LANE = 8, 128
RANK = 32
COPIES = 2
AHEAD = 4
VMEM = 24 * 1024 * 1024


def pieces(value, count):
    parts = []
    for _ in range(count):
        part = value.astype(BF16)
        parts.append(part)
        value = value - part.astype(F32)
    return parts


def dot(a, b, contract, precision=None):
    dims = ((contract[0:1], contract[1:2]), ((), ()))
    return lax.dot_general(a, b, dims, precision=precision, preferred_element_type=F32)


def left_of(shares_ref):
    packed = shares_ref[0]
    for g in range(1, shares_ref.shape[0]):
        packed = packed + shares_ref[g]
    half = LANE // 2
    return jnp.concatenate([packed[:, :half], packed[:, half:]], axis=0)


def project_kernel(own_ref, grads_ref, q_ref, out_ref, grads_buf, sides_ref, q_buf, sems):
    sides_ref[0] = own_ref[0]
    sides_ref[1] = 1 - own_ref[0]
    count = sems.shape[0]
    wide = q_buf.shape[1] // count
    copies = []
    for n in range(count):
        cols = pl.ds(n * wide, wide)
        copies.append(
            (
                pltpu.make_async_copy(grads_ref.at[:, :, cols], grads_buf.at[:, :, cols], sems.at[n, 0]),
                pltpu.make_async_copy(q_ref.at[:, cols], q_buf.at[:, cols], sems.at[n, 1]),
            )
        )
        for copy in copies[-1]:
            copy.start()
    total = None
    for n in range(count):
        for copy in copies[n]:
            copy.wait()
        cols = pl.ds(n * wide, wide)
        stack = jnp.concatenate(pieces(q_buf[:, cols], 2), axis=0)
        part = dot(stack, grads_buf[0, :, cols], (1, 1))
        total = part if total is None else total + part
    local = total[:RANK] + total[RANK:]
    packed = jnp.concatenate([local[: RANK // 2], local[RANK // 2 :]], axis=1)
    for g in range(out_ref.shape[0]):
        out_ref[g] = packed


def project(own, grads, q_prev, groups):
    rows, cols = grads.shape[1:]
    return pl.pallas_call(
        project_kernel,
        in_specs=[pl.BlockSpec(memory_space=pltpu.SMEM)] + [pl.BlockSpec(memory_space=pl.ANY)] * 2,
        out_specs=(
            pl.BlockSpec(memory_space=pltpu.VMEM),
            pl.BlockSpec(memory_space=pltpu.VMEM),
            pl.BlockSpec(memory_space=pltpu.SMEM),
        ),
        out_shape=(
            jax.ShapeDtypeStruct((groups, RANK // 2, LANE), F32),
            pltpu.VMEM(grads.shape, BF16),
            jax.ShapeDtypeStruct((2,), jnp.int32),
        ),
        scratch_shapes=[
            pltpu.VMEM((RANK, cols), F32),
            pltpu.SemaphoreType.DMA((COPIES, 2)),
        ],
        compiler_params=pltpu.CompilerParams(vmem_limit_bytes=VMEM),
        name="project",
    )(own, pltpu.with_memory_space_constraint(grads, pltpu.HBM), pltpu.with_memory_space_constraint(q_prev, pltpu.HBM))


def term_kernel(side, sides_ref, shares_ref, grads_ref, out_ref):
    left = left_of(shares_ref)
    stack = jnp.concatenate(pieces(left, 2), axis=0)
    half = grads_ref.shape[2] // NC
    part = dot(stack, grads_ref[0, :, half_of(side, sides_ref, half)], (1, 0))
    part = part[:RANK] + part[RANK:]
    tiles = out_ref.shape[1] - 1
    wide = dot(left, jnp.concatenate([left] * NX, axis=0), (1, 1), HIGH) / PAIR
    slot = lax.broadcasted_iota(jnp.int32, (SUB, LANE), 1) // RANK
    tile = jnp.zeros((SUB, LANE), F32)
    for x in range(NX):
        tile = jnp.where(slot == x, wide[x * SUB : (x + 1) * SUB], tile)
    for x in range(NX):
        for p in range(NP):
            for t in range(tiles):
                cols = slice((p * tiles + t) * LANE, (p * tiles + t + 1) * LANE)
                out_ref[x * NP + p, t] = part[x * SUB : (x + 1) * SUB, cols]
            out_ref[x * NP + p, tiles] = tile


def term(side, sides, shares, grads):
    rows, cols = grads.shape[1:]
    half = cols // NC
    shape = (NX * NP, half // NP // LANE + 1, SUB, LANE)
    return pl.pallas_call(
        functools.partial(term_kernel, side),
        in_specs=[pl.BlockSpec(memory_space=pltpu.SMEM)] + [pl.BlockSpec(memory_space=pltpu.VMEM)] * 2,
        out_specs=pl.BlockSpec(memory_space=pltpu.VMEM),
        out_shape=jax.ShapeDtypeStruct(shape, F32),
        compiler_params=pltpu.CompilerParams(vmem_limit_bytes=VMEM),
        cost_estimate=pl.CostEstimate(flops=2 * 96 * rows * half, bytes_accessed=6 * rows * half, transcendentals=0),
        name="term",
    )(sides, shares, grads)


def factor_kernel(gram_ref, shares_ref, inverse_ref, basis_ref):
    tile = gram_ref[...]
    lane = lax.broadcasted_iota(jnp.int32, (RANK, LANE), 1)
    row = lax.broadcasted_iota(jnp.int32, (RANK, LANE), 0)
    work = jnp.concatenate([pltpu.roll(tile, (LANE - RANK * x) % LANE, 1) for x in range(NX)], axis=0)
    work = jnp.where(lane < RANK, work, jnp.where(lane - RANK == row, 1.0, 0.0))
    for k in range(0, RANK, AHEAD):
        downs = [jnp.broadcast_to(work[:, j : j + 1], work.shape) for j in range(k, k + AHEAD)]
        rights = [work[j : j + 1] for j in range(k, k + AHEAD)]
        for j in range(AHEAD):
            down = downs[j]
            scale = 1.0 / down[k + j : k + j + 1]
            across = rights[j] * scale
            for i in range(j + 1, AHEAD):
                ratio = down[k + i : k + i + 1]
                rights[i] = rights[i] - ratio * across
                downs[i] = downs[i] - down * (ratio * scale)
            work = jnp.where(row > k + j, work - down * across, work)
    pivots = jnp.sum(jnp.where(lane == row, work, 0.0), axis=1, keepdims=True)
    work = work * (1.0 / jnp.sqrt(pivots))
    inverse = jnp.where(lane < RANK, pltpu.roll(work, LANE - RANK, 1), 0.0)
    one, two = [part.astype(F32) for part in pieces(inverse, 2)]
    one = one + pltpu.roll(one, RANK, 1)
    two = two + pltpu.roll(two, RANK, 1)
    inverse_ref[...] = (one + pltpu.roll(two, 2 * RANK, 1)).astype(BF16)
    basis = dot(left_of(shares_ref), jnp.concatenate([inverse[:, :RANK]] * 4, axis=0), (0, 1), HIGH)
    high = basis.astype(BF16).astype(F32)
    wide = lax.broadcasted_iota(jnp.int32, basis.shape, 1)
    basis_ref[...] = jnp.where(wide < LANE // 2, high, basis - high).astype(BF16)


def factor(gram, shares, rows):
    return pl.pallas_call(
        factor_kernel,
        out_shape=(
            jax.ShapeDtypeStruct((RANK, LANE), BF16),
            jax.ShapeDtypeStruct((rows, LANE), BF16),
        ),
        compiler_params=pltpu.CompilerParams(vmem_limit_bytes=VMEM),
        cost_estimate=pl.CostEstimate(flops=1 << 22, bytes_accessed=1 << 20, transcendentals=32),
        name="factor",
    )(gram, shares)


def solve(total_ref, inverse_ref, groups):
    tiles = total_ref.shape[1]
    columns = []
    for t in range(NP * tiles):
        parts = [total_ref[x * NP + t // tiles, t % tiles] for x in range(NX)]
        columns.append(jnp.concatenate(parts, axis=0))
    one, two = pieces(jnp.concatenate(columns, axis=1), 2)
    return dot(inverse_ref[...], jnp.concatenate([one, two, one, two], axis=0), (1, 0)) / groups


def residual(q_new, basis_ref, grads):
    high, low = pieces(q_new, 2)
    approx = dot(basis_ref[...], jnp.concatenate([high, low, high, low], axis=0), (1, 0))
    return (grads.astype(F32) - approx).astype(BF16)


def half_of(side, sides_ref, half):
    return pl.ds(pl.multiple_of(sides_ref[side] * half, LANE), half)


def mine_kernel(groups, sides_ref, total_ref, inverse_ref, basis_ref, grads_ref, q_ref, resid_ref, q_buf, sem):
    here = half_of(0, sides_ref, q_buf.shape[1])
    q_new = solve(total_ref, inverse_ref, groups)
    q_buf[...] = q_new
    copy = pltpu.make_async_copy(q_buf, q_ref.at[:, here], sem)
    copy.start()
    resid_ref[0] = residual(q_new, basis_ref, grads_ref[0, :, here])
    copy.wait()


def mine(sides, total, inverse, basis, grads, groups):
    rows, cols = grads.shape[1:]
    half = cols // NC
    return pl.pallas_call(
        functools.partial(mine_kernel, groups),
        in_specs=[pl.BlockSpec(memory_space=pltpu.SMEM)] + [pl.BlockSpec(memory_space=pltpu.VMEM)] * 4,
        out_specs=(pl.BlockSpec(memory_space=pl.ANY), pl.BlockSpec(memory_space=pltpu.VMEM)),
        out_shape=(pltpu.HBM((RANK, cols), F32), pltpu.VMEM((1, rows, half), BF16)),
        scratch_shapes=[pltpu.VMEM((RANK, half), F32), pltpu.SemaphoreType.DMA],
        compiler_params=pltpu.CompilerParams(vmem_limit_bytes=VMEM),
        cost_estimate=pl.CostEstimate(flops=2 * 160 * rows * half, bytes_accessed=6 * rows * half, transcendentals=0),
        name="mine",
    )(sides, total, inverse, basis, grads)


def finish_kernel(
    groups, sides_ref, total_ref, inverse_ref, basis_ref, grads_ref, mine_q_ref, mine_resid_ref,
    q_ref, resid_ref, q_buf, resid_buf, sems,
):
    half = q_buf.shape[1]
    here, there = half_of(0, sides_ref, half), half_of(1, sides_ref, half)
    copies = [
        pltpu.make_async_copy(mine_resid_ref, resid_ref.at[:, :, here], sems.at[0]),
        pltpu.make_async_copy(q_buf, q_ref.at[:, there], sems.at[1]),
        pltpu.make_async_copy(resid_buf, resid_ref.at[:, :, there], sems.at[2]),
    ]
    copies[0].start()
    q_new = solve(total_ref, inverse_ref, groups)
    q_buf[...] = q_new
    copies[1].start()
    resid_buf[0] = residual(q_new, basis_ref, grads_ref[0, :, there])
    copies[2].start()
    for copy in copies:
        copy.wait()


def finish(sides, total, inverse, basis, grads, groups, done):
    rows, cols = grads.shape[1:]
    half = cols // NC
    return pl.pallas_call(
        functools.partial(finish_kernel, groups),
        in_specs=[pl.BlockSpec(memory_space=pltpu.SMEM)] + [pl.BlockSpec(memory_space=pltpu.VMEM)] * 4
        + [pl.BlockSpec(memory_space=pl.ANY), pl.BlockSpec(memory_space=pltpu.VMEM)],
        out_specs=(pl.BlockSpec(memory_space=pl.ANY),) * 2,
        out_shape=(
            jax.ShapeDtypeStruct((RANK, cols), F32),
            jax.ShapeDtypeStruct((1, rows, cols), BF16),
        ),
        scratch_shapes=[
            pltpu.VMEM((RANK, half), F32),
            pltpu.VMEM((1, rows, half), BF16),
            pltpu.SemaphoreType.DMA((3,)),
        ],
        input_output_aliases={5: 0},
        compiler_params=pltpu.CompilerParams(vmem_limit_bytes=VMEM),
        name="finish",
    )(sides, total, inverse, basis, grads, *done)


def exchange(blocks, axis):
    return lax.all_to_all(blocks, axis, 0, 0, tiled=True)


def spread(block, axis):
    return exchange(jnp.broadcast_to(block[None], (lax.axis_size(axis),) + block.shape), axis)


def per_device(grads, q_prev):
    groups = lax.axis_size(("far", "near"))
    swap = [(0, 1), (1, 0)]
    own = lax.axis_index("c").astype(jnp.int32).reshape(1)

    shares, grads, sides = project(own, grads, q_prev, groups)
    shares = exchange(shares, ("far", "near"))
    away = lax.ppermute(term(1, sides, shares, grads), "c", swap)
    part = term(0, sides, shares, grads) + away
    part = jnp.sum(exchange(part, ("x", "near", "side")), axis=0)
    part = jnp.sum(spread(part, "y"), axis=0)
    gram = part[-1]
    part = jnp.sum(spread(part[:-1], "far"), axis=0)
    total = spread(part, ("x", "near", "side"))
    away = lax.ppermute(total, "c", swap)
    inverse, basis = factor(gram, shares, grads.shape[1])
    done = mine(sides, total, inverse, basis, grads, groups)
    return tuple(finish(sides, away, inverse, basis, grads, groups, done))


def solution(mesh):
    groups = mesh.devices.shape[1]
    shape = (NY, PAIR, NX, NC, groups // PAIR, PAIR)
    fine = Mesh(mesh.devices.reshape(shape), ("y", "side", "x", "c", "far", "near"))
    split = P(("far", "near"), ("y", "side", "x", "c"), None)
    return jax.shard_map(per_device, mesh=fine, in_specs=(split, P()), out_specs=(P(), split), check_vma=False)
```
